256 devices in a mesh: tp: 8 (over z_hi, x), sp: 32 (over y, z_lo, core).
Axes of the slice: x: 4, y: 4, z: 8 (z_hi: 2, z_lo: 4; z = z_hi * 4 + z_lo), core: 2. Of those that a mesh axis runs over, the one named last changes fastest.
Arguments:
- enc_rows: bfloat16 [384, 4096], P('tp', 'sp'), may hold values from -6 to 6
- enc_gain: float32 [4096], P('sp'), may hold values from 0.1 to 1.9
- w_gate: bfloat16 [4096, 14336], P('sp', 'tp'), may hold values from -0.09375 to 0.09375
- w_up: bfloat16 [4096, 14336], P('sp', 'tp'), may hold values from -0.09375 to 0.09375
- w_down: bfloat16 [14336, 4096], P('tp', 'sp'), may hold values from -0.046875 to 0.046875
- w_text_kv: bfloat16 [4096, 24, 2, 128], P('sp', 'tp'), may hold values from -0.09375 to 0.09375
- text_gain: float32 [128], replicated, may hold values from 0.8 to 2.2
- vid_rows: bfloat16 [12288, 3072], P('sp', 'tp'), may hold values from -6 to 6
- mod_shift: float32 [3072], replicated, may hold values from -3 to 3
- mod_scale: float32 [3072], replicated, may hold values from -3 to 3
- w_qkv: bfloat16 [3072, 24, 3, 128], P(None, 'tp')
- q_gain: float32 [128], replicated, may hold values from 0.8 to 4.5
- k_gain: float32 [128], replicated, may hold values from 0.8 to 4.5
Outputs:
- enc_out: bfloat16 [384, 4096], P('tp', 'sp')
- attn_out: bfloat16 [12288, 24, 128], P('sp', 'tp')
The draws below stay inside these ranges and needn't reach their ends.
All inputs are finite; a program needn't handle non-finite values.
Results may differ from the reference program's by a relative error of at most 0.014.
The reference program's roundings to bfloat16 on the way count: a program that leaves them out, or rounds other values in their place, can miss the bound.
Values may be sent and summed in bfloat16 or wider, within the bound.
No kernel may reach another device: no remote copies, remote signals or barrier semaphores. Data moves between devices by JAX's collectives and lax.ppermute only.
A program may use at most 128 MiB of HBM per device.

```python
import math
import jax
import jax.numpy as jnp
from jax import lax

D = 4096
FF = 14336
DM = 3072
HEADS = 24
HD = 128
ETOK = 384
VTOK = 12288


def draw_w_qkv(key, part):
    key = jax.random.fold_in(key, 11)
    base = jax.random.normal(key, (DM, HEADS, 3, HD), jnp.float32) * DM ** (-0.5)
    return base.astype(jnp.bfloat16)


def spread_gain(key, lower, upper):
    return jnp.exp(jax.random.uniform(key, (HD,), jnp.float32, math.log(lower), math.log(upper)))


def draw_q_gain(key, part):
    key = jax.random.fold_in(key, 12)
    return spread_gain(key, 0.8, 2.2)


def draw_k_gain(key, part):
    key = jax.random.fold_in(key, 13)
    return spread_gain(key, 0.8, 2.2)


def levels(own_key, shape, cuts, least, largest):
    def one(axis_at, blocks):
        heights = jax.random.uniform(jax.random.fold_in(jax.random.fold_in(own_key, 6), axis_at), (blocks,), jnp.float32, least / len(cuts), largest / len(cuts))
        return jnp.repeat(jnp.exp(heights), shape[axis_at] // blocks).reshape((-1,) + (1,) * (len(shape) - axis_at - 1))

    loudness = one(*cuts[0])
    for cut in cuts[1:]:
        loudness = loudness * one(*cut)
    return loudness


def scatter_about(own_key, extent, deviation, bound, split=(), dtype=jnp.bfloat16):
    level = levels(own_key, extent, split, -0.22, 0.18) if split else 1.0
    values = jax.random.normal(own_key, extent, jnp.float32) * deviation * level
    return jnp.minimum(jnp.maximum(values, -bound), bound).astype(dtype)


def setup_inputs(seed: int = 0) -> dict:
    arg_keys = jax.random.split(jax.random.key(seed), 14)
    return {
        "enc_rows": scatter_about(arg_keys[0], (ETOK, D), 1.0, 6.0, ((0, 8), (1, 32))),
        "enc_gain": jnp.clip(1.0 + 0.18 * jax.random.normal(arg_keys[1], (D,), jnp.float32), 0.1, 1.9),
        "w_gate": scatter_about(arg_keys[2], (D, FF), D ** -0.5, 0.09375, ((0, 32), (1, 8))),
        "w_up": scatter_about(arg_keys[3], (D, FF), D ** -0.5, 0.09375, ((0, 32), (1, 8))),
        "w_down": scatter_about(arg_keys[4], (FF, D), FF ** -0.5, 0.046875, ((0, 8), (1, 32))),
        "w_text_kv": scatter_about(arg_keys[5], (D, HEADS, 2, HD), D ** -0.5, 0.09375, ((0, 32), (1, 8))),
        "text_gain": jnp.clip(jnp.exp(jax.random.uniform(arg_keys[6], (HD,), jnp.float32, math.log(0.8), math.log(2.2))), 0.8, 2.2),
        "vid_rows": scatter_about(arg_keys[7], (VTOK, DM), 1.0, 6.0, ((0, 32), (1, 8))),
        "mod_shift": scatter_about(arg_keys[8], (DM,), 0.5, 3.0, (), jnp.float32),
        "mod_scale": scatter_about(arg_keys[9], (DM,), 0.5, 3.0, (), jnp.float32),
        "w_qkv": draw_w_qkv(jax.random.fold_in(arg_keys[13], 71), 0),
        "q_gain": draw_q_gain(jax.random.fold_in(arg_keys[13], 71), 0),
        "k_gain": draw_k_gain(jax.random.fold_in(arg_keys[13], 71), 0),
    }


def rms_rows(values, gain):
    return values * lax.rsqrt(lax.optimization_barrier(jnp.mean(values * values, axis=-1, keepdims=True)) + 1e-06) * gain

def one_head(inputs):
    queries, keys, values = inputs
    query_count = queries.shape[0]
    block = math.gcd(query_count, 2048)
    query_blocks = queries.reshape(query_count // block, block, queries.shape[1])

    def one_block(query_block):
        scores = jnp.dot(query_block, keys.T, preferred_element_type=jnp.float32) / jnp.sqrt(jnp.float32(HD))
        row_max = lax.optimization_barrier(jnp.max(scores, axis=-1, keepdims=True))
        expon = jnp.exp(scores - row_max)
        denominator = lax.optimization_barrier(jnp.sum(expon, axis=-1, keepdims=True))
        weights = expon.astype(jnp.bfloat16)
        return jnp.dot(weights, values, preferred_element_type=jnp.float32) / denominator
    result = lax.map(one_block, query_blocks)
    return result.reshape(query_count, values.shape[1])

def reference(enc_rows, enc_gain, w_gate, w_up, w_down, w_text_kv, text_gain, vid_rows, mod_shift, mod_scale, w_qkv, q_gain, k_gain):
    rows_float = enc_rows.astype(jnp.float32)
    row_power = lax.optimization_barrier(jnp.sum(rows_float * rows_float, axis=1))
    scaled = (rows_float * enc_gain).astype(jnp.bfloat16)
    inv_rms = lax.rsqrt(row_power / D + 1e-05)[:, None]
    gate_value = jnp.dot(scaled, w_gate, preferred_element_type=jnp.float32) * inv_rms
    up_value = jnp.dot(scaled, w_up, preferred_element_type=jnp.float32) * inv_rms
    hidden = (jax.nn.silu(gate_value) * up_value).astype(jnp.bfloat16)
    enc_out = (rows_float + jnp.dot(hidden, w_down, preferred_element_type=jnp.float32)).astype(jnp.bfloat16)
    text_kv = jnp.dot(enc_out, w_text_kv.reshape(D, HEADS * 2 * HD), preferred_element_type=jnp.float32)
    text_kv = text_kv.reshape(ETOK, HEADS, 2, HD)
    text_key = rms_rows(text_kv[:, :, 0], text_gain).astype(jnp.bfloat16)
    text_value = text_kv[:, :, 1].astype(jnp.bfloat16)
    video_float = vid_rows.astype(jnp.float32)
    row_mean = lax.optimization_barrier(jnp.mean(video_float, axis=1, keepdims=True))
    centred = video_float - row_mean
    row_var = lax.optimization_barrier(jnp.mean(centred * centred, axis=1, keepdims=True))
    modulated = (centred * lax.rsqrt(row_var + 1e-06) * (1.0 + mod_scale) + mod_shift).astype(jnp.bfloat16)
    projected = jnp.dot(modulated, w_qkv.reshape(DM, HEADS * 3 * HD), preferred_element_type=jnp.float32)
    projected = projected.reshape(VTOK, HEADS, 3, HD)
    queries = rms_rows(projected[:, :, 0], q_gain).astype(jnp.bfloat16)
    video_keys = rms_rows(projected[:, :, 1], k_gain).astype(jnp.bfloat16)
    video_values = projected[:, :, 2].astype(jnp.bfloat16)
    all_keys = jnp.concatenate([text_key, video_keys], axis=0)
    all_values = jnp.concatenate([text_value, video_values], axis=0)
    per_head = lax.map(one_head, (jnp.transpose(queries, (1, 0, 2)), jnp.transpose(all_keys, (1, 0, 2)), jnp.transpose(all_values, (1, 0, 2))))
    attn_out = jnp.transpose(per_head, (1, 0, 2)).astype(jnp.bfloat16)
    return (enc_out, attn_out)
```

```python
import functools
import math

import jax
import jax.numpy as jnp
from jax import lax
from jax.experimental import pallas as pl
from jax.experimental.pallas import tpu as pltpu
from jax.sharding import PartitionSpec as P

D = 4096
BF = jnp.bfloat16
F32 = jnp.float32
HD = 128
LOG2E = 1.4426950408889634


def sp_send(value, dy=0, dz=0, dc=0):
    pairs = []
    for i in range(32):
        y, z, c = i // 8, (i // 2) % 4, i % 2
        pairs.append((i, (((y + dy) % 4) * 4 + (z + dz) % 4) * 2 + (c + dc) % 2))
    return lax.ppermute(value, "sp", pairs)


def tp_send(value, dh=0, dx=0):
    pairs = [(i, ((i // 4 + dh) % 2) * 4 + (i % 4 + dx) % 4) for i in range(8)]
    return lax.ppermute(value, "tp", pairs)


def qkv_kernel(order, *refs):
    blocks, (scale, shift, weight, q_gain, k_gain, q_out, kv_out, modulated) = refs[:8], refs[8:]
    width = blocks[0].shape[1]
    total = 8 * width
    row_sum = 0.0
    for block in blocks:
        row_sum = row_sum + jnp.sum(block[...].astype(F32), axis=1, keepdims=True)
    mean = row_sum / total
    square_sum = 0.0
    for block in blocks:
        centred = block[...].astype(F32) - mean
        square_sum = square_sum + jnp.sum(centred * centred, axis=1, keepdims=True)
    inverse = lax.rsqrt(square_sum / total + 1e-06)
    for k, block in enumerate(blocks):
        at = order[k]
        gain = 1.0 + scale[pl.ds(at, 1), :]
        value = (block[...].astype(F32) - mean) * inverse * gain + shift[pl.ds(at, 1), :]
        modulated[:, pl.ds(pl.multiple_of(at * width, width), width)] = value.astype(BF)
    projected = jnp.dot(modulated[...], weight[...], preferred_element_type=F32)
    for h in range(3):
        for s in range(3):
            part = projected[:, (3 * h + s) * HD : (3 * h + s + 1) * HD]
            if s < 2:
                gain = (q_gain if s == 0 else k_gain)[...]
                part = part * lax.rsqrt(jnp.mean(part * part, axis=-1, keepdims=True) + 1e-06) * gain
            if s == 0:
                q_out[:, h * HD : (h + 1) * HD] = part.astype(BF)
            else:
                at = (s - 1) * 3 + h
                kv_out[:, at * HD : (at + 1) * HD] = part.astype(BF)


def qkv(order, blocks, scale, shift, weight, q_gain, k_gain):
    rows, width = blocks[0].shape
    depth, columns = weight.shape
    tile = 128
    whole = lambda shape: pl.BlockSpec(shape, lambda i, o: (0,) * len(shape))
    return pl.pallas_call(
        qkv_kernel,
        grid_spec=pltpu.PrefetchScalarGridSpec(
            num_scalar_prefetch=1,
            grid=(rows // tile,),
            in_specs=[pl.BlockSpec((tile, width), lambda i, o: (i, 0))] * 8
            + [whole((8, width)), whole((8, width)), whole((depth, columns)), whole((1, HD)), whole((1, HD))],
            out_specs=[
                pl.BlockSpec((tile, 3 * HD), lambda i, o: (i, 0)),
                pl.BlockSpec((tile, 6 * HD), lambda i, o: (i, 0)),
            ],
            scratch_shapes=[pltpu.VMEM((tile, depth), BF)],
        ),
        out_shape=[jax.ShapeDtypeStruct((rows, 3 * HD), BF), jax.ShapeDtypeStruct((rows, 6 * HD), BF)],
        compiler_params=pltpu.CompilerParams(vmem_limit_bytes=40 * 2**20),
        cost_estimate=pl.CostEstimate(
            flops=2 * rows * depth * columns, bytes_accessed=2 * (depth * columns + 2 * rows * depth), transcendentals=0
        ),
        name="qkv",
    )(order, *blocks, scale, shift, weight, q_gain, k_gain)


def attend_tile(query, pieces):
    top = total = out = None
    for keys, values in pieces:
        scores = lax.dot_general(query, keys, (((1,), (1,)), ((), ())), preferred_element_type=F32)
        here = jnp.max(scores, axis=1, keepdims=True)
        new_top = here if top is None else jnp.maximum(top, here)
        expon = jnp.exp2(scores - new_top)
        piece_sum = jnp.sum(expon, axis=1, keepdims=True)
        piece_out = jnp.dot(expon.astype(BF), values, preferred_element_type=F32)
        if top is None:
            total, out = piece_sum, piece_out
        else:
            factor = jnp.exp2(top - new_top)
            total, out = total * factor + piece_sum, out * factor + piece_out
        top = new_top
    return top, total, out


def attend_kernel(query_ref, key_ref, value_ref, out_ref, *, tile, piece):
    rows = query_ref.shape[0]
    count = key_ref.shape[0]
    for r in range(rows // tile):
        query = query_ref[r * tile : (r + 1) * tile, :]
        pieces = [
            (key_ref[k * piece : (k + 1) * piece, :], value_ref[k * piece : (k + 1) * piece, :])
            for k in range(count // piece)
        ]
        top, total, out = attend_tile(query, pieces)
        out_ref[r * tile : (r + 1) * tile, :] = (out / total).astype(BF)
        level = top + jnp.log2(total)
        across = jnp.transpose(jnp.broadcast_to(level, (tile, HD)))[0:8, :]
        high = across.astype(BF).astype(F32)
        low = across - high
        row_at = lax.broadcasted_iota(jnp.int32, (16, tile), 0)
        both = jnp.concatenate([high, high], axis=0)
        both = jnp.where(row_at == 1, jnp.concatenate([low, low], axis=0), both)
        out_ref[rows + 16 * r : rows + 16 * (r + 1), :] = both.astype(BF)


def attend(query, pairs):
    rows = query.shape[0]
    count = pairs.shape[0]
    tile = 128
    out_rows = rows + 16 * (rows // tile)
    return pl.pallas_call(
        functools.partial(attend_kernel, tile=tile, piece=1024),
        grid=(3,),
        in_specs=[
            pl.BlockSpec((rows, HD), lambda h: (0, h)),
            pl.BlockSpec((count, HD), lambda h: (0, h)),
            pl.BlockSpec((count, HD), lambda h: (0, 3 + h)),
        ],
        out_specs=pl.BlockSpec((out_rows, HD), lambda h: (0, h)),
        out_shape=jax.ShapeDtypeStruct((out_rows, 3 * HD), BF),
        compiler_params=pltpu.CompilerParams(vmem_limit_bytes=40 * 2**20),
        cost_estimate=pl.CostEstimate(
            flops=12 * rows * count * HD, bytes_accessed=12 * count * HD, transcendentals=3 * rows * count
        ),
        name="attend",
    )(query, pairs, pairs)


def combine_kernel(query_ref, key_ref, value_ref, *refs):
    parts, out_ref = refs[:-1], refs[-1]
    rows = query_ref.shape[0]
    tile = 128
    for r in range(rows // tile):
        query = query_ref[r * tile : (r + 1) * tile, :]
        top, total, out = attend_tile(query, [(key_ref[...], value_ref[...])])
        levels = []
        for part in parts:
            both = part[rows + 16 * r : rows + 16 * (r + 1), :].astype(F32)
            row_level = both[0:1, :] + both[1:2, :]
            levels.append(jnp.transpose(jnp.broadcast_to(row_level, (HD, tile))))
        new_top = top
        for level in levels:
            new_top = jnp.maximum(new_top, level)
        factor = jnp.exp2(top - new_top)
        total, out = total * factor, out * factor
        for part, level in zip(parts, levels):
            weight = jnp.exp2(level - new_top)
            total = total + weight
            out = out + weight * part[r * tile : (r + 1) * tile, :].astype(F32)
        out_ref[r * tile : (r + 1) * tile, :] = (out / total).astype(BF)


def combine(query, text, parts):
    rows = query.shape[0]
    count = text.shape[0]
    part_rows = parts[0].shape[0]
    return pl.pallas_call(
        combine_kernel,
        grid=(3,),
        in_specs=[
            pl.BlockSpec((rows, HD), lambda h: (0, h)),
            pl.BlockSpec((count, HD), lambda h: (0, h)),
            pl.BlockSpec((count, HD), lambda h: (0, 3 + h)),
        ]
        + [pl.BlockSpec((part_rows, HD), lambda h: (0, h))] * len(parts),
        out_specs=pl.BlockSpec((rows, HD), lambda h: (0, h)),
        out_shape=jax.ShapeDtypeStruct((rows, 3 * HD), BF),
        cost_estimate=pl.CostEstimate(
            flops=12 * rows * count * HD, bytes_accessed=6 * 8 * rows * HD, transcendentals=3 * rows * count
        ),
        name="combine",
    )(query, text, text, *parts)


def take(stack, at):
    return lax.dynamic_index_in_dim(stack, at, 0, keepdims=False)


def shards(
    enc_rows,
    enc_gain,
    w_gate,
    w_up,
    w_down,
    w_text_kv,
    text_gain,
    vid_rows,
    mod_shift,
    mod_scale,
    w_qkv,
    q_gain,
    k_gain,
):
    tp = lax.axis_index("tp")
    sp = lax.axis_index("sp")
    hi, x = tp // 4, tp % 4
    y, z, core = sp // 8, (sp // 2) % 4, sp % 2

    half = enc_rows.shape[0] // 2
    halves = enc_rows.reshape(2, half, -1)
    mine = take(halves, core)
    other = sp_send(take(halves, 1 - core), dc=1)
    rows_c = jnp.concatenate([mine, other], axis=1)
    rows_h = jnp.stack([rows_c, tp_send(rows_c, dh=1)])
    rows_x = jnp.stack([rows_h] + [tp_send(rows_h, dx=-j) for j in (1, 2, 3)])
    features = rows_x.shape[-1]
    rows_x = rows_x.reshape(-1, features)
    rows_y = jnp.concatenate([rows_x] + [sp_send(rows_x, dy=-j) for j in (1, 2, 3)], axis=1)

    from_h = tp_send(vid_rows, dh=1)
    blocks = [vid_rows] + [tp_send(vid_rows, dx=-j) for j in (1, 2, 3)]
    blocks += [from_h] + [tp_send(from_h, dx=-j) for j in (1, 2, 3)]
    order = jnp.stack([(hi ^ a) * 4 + (x + j) % 4 for a in (0, 1) for j in range(4)]).astype(jnp.int32)

    depth, units = w_gate.shape
    own_units = units // 4
    gained = [(w.astype(F32) * enc_gain[:, None]).astype(BF) for w in (w_gate, w_up)]

    def unit_columns(w, at):
        return lax.dynamic_slice_in_dim(w, at * own_units, own_units, 1)

    def gate_up(j):
        at = (y - j) % 4
        return jnp.concatenate([unit_columns(w, at) for w in gained], axis=1)

    own_gu = jnp.stack([gate_up(0)] + [sp_send(gate_up(j), dy=-j) for j in (1, 2, 3)])
    both_gu = jnp.stack([own_gu, sp_send(own_gu, dc=1)], axis=1).reshape(-1, 2 * own_units)
    padded = (own_units + 127) // 128 * 128
    pad = ((0, 0), (0, padded - own_units))
    both_gu = jnp.concatenate([jnp.pad(both_gu[:, :own_units], pad), jnp.pad(both_gu[:, own_units:], pad)], axis=1)

    def down_rows(j):
        return lax.dynamic_slice_in_dim(w_down, (y - j) % 4 * own_units, own_units, 0)

    own_down = jnp.stack([down_rows(0)] + [sp_send(down_rows(j), dy=-j) for j in (1, 2, 3)])
    both_down = jnp.stack([own_down, sp_send(own_down, dc=1)], axis=1)
    both_down = jnp.transpose(both_down, (2, 0, 1, 3)).reshape(own_units, -1)
    both_down = jnp.pad(both_down, ((0, padded - own_units), (0, 0)))

    own_text = jnp.transpose(w_text_kv, (0, 2, 1, 3)).reshape(w_text_kv.shape[0], -1)
    both_text = jnp.concatenate([own_text, sp_send(own_text, dc=1)], axis=0)

    flat_qkv = w_qkv.reshape(w_qkv.shape[0], -1)
    query, pairs = qkv(
        order,
        blocks,
        mod_scale.reshape(8, -1),
        mod_shift.reshape(8, -1),
        flat_qkv,
        (q_gain * (LOG2E / math.sqrt(HD)))[None],
        k_gain[None],
    )
    groups = [[(yy * 4 + zz) * 2 + cc for yy in range(4) for cc in range(2)] for zz in range(4)]
    all_pairs = lax.all_gather(pairs, "sp", axis=0, tiled=True, axis_index_groups=groups)
    parts = []
    for j in (2, 1, 3):
        far_query = sp_send(query, dz=-j)
        parts.append(sp_send(attend(far_query, all_pairs), dz=j))
    parts.append(attend(query, all_pairs))

    gate_up_part = jnp.dot(rows_y, both_gu, preferred_element_type=F32)
    rows_float = rows_y.astype(F32)
    power = jnp.sum(rows_float * rows_float, axis=1, keepdims=True)
    power_high = lax.reduce_precision(power, 8, 7)
    power_low = power - power_high
    column = lax.broadcasted_iota(jnp.int32, gate_up_part.shape, 1)
    gate_up_part = jnp.where(column == own_units, power_high, gate_up_part)
    gate_up_part = jnp.where(column == own_units + 1, power_low, gate_up_part)
    gate_up_part = gate_up_part.reshape(4, 2 * half, -1)
    gate_up_sent = gate_up_part.astype(BF)
    gate_up_sum = take(gate_up_part, z)
    for j in (2, 1, 3):
        gate_up_sum = gate_up_sum + sp_send(take(gate_up_sent, (z + j) % 4), dz=j).astype(F32)
    row_power = gate_up_sum[:, own_units : own_units + 1] + gate_up_sum[:, own_units + 1 : own_units + 2]
    inv_rms = lax.rsqrt(row_power / D + 1e-05)
    gate, up = gate_up_sum[:, :padded] * inv_rms, gate_up_sum[:, padded:] * inv_rms
    column = lax.broadcasted_iota(jnp.int32, gate.shape, 1)
    hidden = jnp.where(column < own_units, jax.nn.silu(gate) * up, 0.0).astype(BF)
    hidden = jnp.concatenate([hidden] + [sp_send(hidden, dz=-j) for j in (1, 2, 3)], axis=0)

    down_part = jnp.dot(hidden, both_down, preferred_element_type=F32)
    down_sent = down_part.astype(BF)
    down = down_part[:, :features]
    for j in (2, 1, 3):
        down = down + sp_send(down_sent[:, j * features : (j + 1) * features], dy=j).astype(F32)
    from_other = tp_send(down.astype(BF), dh=1).reshape(4, 2, half, features)
    down = down.reshape(4, 2, half, features) + from_other[:, ::-1].astype(F32)
    down_sent = down.astype(BF)
    for j in (2, 1, 3):
        down = down + jnp.roll(tp_send(down_sent, dx=-j).astype(F32), j, axis=0)
    turned = rows_x.reshape(4, 2, half, features)
    turned = lax.dynamic_slice_in_dim(jnp.concatenate([turned, turned], axis=0), z, 4, 0)
    enc_full = (turned.astype(F32) + down).astype(BF)

    own_out = take(enc_full, (4 - z) % 4)[0]
    own_part, far_part = own_out[:, : features // 2], own_out[:, features // 2 :]
    far_part = sp_send(far_part, dc=1)
    enc_mine = jnp.where(
        core == 0,
        jnp.concatenate([own_part, far_part], axis=0),
        jnp.concatenate([far_part, own_part], axis=0),
    )

    text_part = jnp.dot(enc_full.reshape(-1, features), both_text, preferred_element_type=F32)
    text_part = text_part.reshape(4, 2 * half, -1)
    text_sent = text_part.astype(BF)
    text = take(text_part, (y - z) % 4)
    for j in (2, 1, 3):
        text = text + sp_send(take(text_sent, (y + j - z) % 4), dy=j).astype(F32)
    text_sent = text.astype(BF)
    for j in (2, 1, 3):
        text = text + sp_send(text_sent, dz=j).astype(F32)
    text = text.reshape(2 * half, 2, 3, HD)
    text_key = text[:, 0]
    text_key = text_key * lax.rsqrt(jnp.mean(text_key * text_key, axis=-1, keepdims=True) + 1e-06) * text_gain
    text = jnp.stack([text_key, text[:, 1]], axis=1).astype(BF).reshape(2 * half, -1)
    text = jnp.concatenate([text] + [sp_send(text, dy=-j) for j in (1, 2, 3)], axis=0)
    text = jnp.concatenate([text, sp_send(text, dc=1)], axis=0)

    out = combine(query, text, parts)
    return (enc_mine, out.reshape(out.shape[0], 3, HD))


def solution(mesh):
    in_specs = (
        P("tp", "sp"),
        P("sp"),
        P("sp", "tp"),
        P("sp", "tp"),
        P("tp", "sp"),
        P("sp", "tp", None, None),
        P(),
        P("sp", "tp"),
        P(),
        P(),
        P(None, "tp", None, None),
        P(),
        P(),
    )
    out_specs = (P("tp", "sp"), P("sp", "tp", None))
    return jax.shard_map(shards, mesh=mesh, in_specs=in_specs, out_specs=out_specs, check_vma=False)
```

```python
import functools
import math

import jax
import jax.numpy as jnp
from jax import lax
from jax.experimental import pallas as pl
from jax.experimental.pallas import tpu as pltpu
from jax.sharding import PartitionSpec as P

D = 4096
BF = jnp.bfloat16
F32 = jnp.float32
HD = 128
LOG2E = 1.4426950408889634


def sp_send(value, dy=0, dz=0, dc=0):
    pairs = []
    for i in range(32):
        y, z, c = i // 8, (i // 2) % 4, i % 2
        pairs.append((i, (((y + dy) % 4) * 4 + (z + dz) % 4) * 2 + (c + dc) % 2))
    return lax.ppermute(value, "sp", pairs)


def tp_send(value, dh=0, dx=0):
    pairs = [(i, ((i // 4 + dh) % 2) * 4 + (i % 4 + dx) % 4) for i in range(8)]
    return lax.ppermute(value, "tp", pairs)


def glance(array):
    return pl.BlockSpec((1,) * (array.ndim - 2) + (16, HD), lambda *i: (0,) * array.ndim)


def call(kernel, outs, ins, after=(), scalars=None, scratch=(), flops=0, name="step", stream=False):
    count = len(ins)
    shapes = [jax.ShapeDtypeStruct(shape, dtype) for shape, dtype in outs]
    lead = [] if scalars is None else [scalars]

    def body(*refs):
        kept = refs[: len(lead) + count] + refs[len(lead) + count + len(after) :]
        kernel(*kept)

    size = sum(math.prod(a.shape) * a.dtype.itemsize for a in list(ins) + shapes)
    return pl.pallas_call(
        body,
        grid=(1,),
        in_specs=[pl.BlockSpec(memory_space=pltpu.SMEM)] * len(lead)
        + [
            pl.BlockSpec(a.shape, lambda i, n=len(a.shape): (0,) * n) if stream else pl.BlockSpec(memory_space=pltpu.VMEM)
            for a in ins
        ]
        + [glance(a) for a in after],
        out_specs=[pl.BlockSpec(memory_space=pltpu.VMEM)] * len(shapes),
        out_shape=shapes,
        scratch_shapes=list(scratch),
        compiler_params=pltpu.CompilerParams(vmem_limit_bytes=(60 if stream else 24) * 2**20),
        cost_estimate=pl.CostEstimate(flops=flops, bytes_accessed=size, transcendentals=0),
        name=name,
    )(*lead, *ins, *after)


UNITS = 448
WINDOW = 512
PAYLOAD = 8 * HD + WINDOW


def prepare_kernel(place, gate, up, down, gain, text, out0, out1, out2, out3, out_text):
    gain_column = gain[...]
    lane = lax.broadcasted_iota(jnp.int32, (HD, WINDOW), 1)
    row = lax.broadcasted_iota(jnp.int32, (WINDOW, HD), 0)
    for j, out in enumerate((out0, out1, out2, out3)):
        at = lax.rem(place[0] + 4 - j, 4)
        skip = lax.rem(at, 2) * 64
        start = pl.multiple_of(at * UNITS - skip, HD)
        for side, weight in enumerate((gate, up)):
            value = weight[:, pl.ds(start, WINDOW)].astype(F32) * gain_column
            value = jnp.where((lane >= skip) & (lane < skip + UNITS), value, 0.0).astype(BF)
            for p in range(4):
                out[(4 * side + p) * HD : (4 * side + p + 1) * HD, :] = value[:, p * HD : (p + 1) * HD]
        value = down[pl.ds(start, WINDOW), :].astype(F32)
        value = jnp.where((row >= skip) & (row < skip + UNITS), value, 0.0)
        out[8 * HD :, :] = value.astype(BF)
    for s in range(2):
        for h in range(3):
            out_text[(3 * s + h) * HD : (3 * s + h + 1) * HD, :] = text[:, h, s, :]


def join_rows_kernel(*refs):
    out = refs[-1]
    at = 0
    for ref in refs[:-1]:
        out[at : at + ref.shape[0], :] = ref[...]
        at += ref.shape[0]


def copy_kernel(source, out):
    out[...] = source[...]


def first_kernel(video, own, out):
    rows = video.shape[0]
    out[0:rows, :] = video[...]
    for k in range(3):
        out[rows:, k * HD : (k + 1) * HD] = own[16 * k : 16 * (k + 1), :]


def pick_kernel(place, *refs):
    blocks, weights, (mine, other, weights_out) = refs[:8], refs[8:-3], refs[-3:]
    rows = blocks[0].shape[0] - 16
    first, second = [], []
    for j in range(4):
        for a in range(2):
            tail = blocks[a * 4 + j][rows:, :].astype(F32)
            part = jnp.concatenate([tail[:, k * HD : (k + 1) * HD] for k in range(3)], axis=0)
            first.append(part[:24])
            second.append(part[24:])
    first, second = jnp.concatenate(first, axis=0), jnp.concatenate(second, axis=0)
    is_first = place[2] == 0
    mine[...] = jnp.where(is_first, first, second).astype(BF)
    other[...] = jnp.where(is_first, second, first).astype(BF)
    join_rows_kernel(*weights, weights_out)


def join_columns_kernel(left, right, out):
    out[:, : left.shape[1]] = left[...]
    out[:, left.shape[1] :] = right[...]


def weight_columns(ref, at, count):
    return jnp.concatenate([ref[at + p * HD : at + (p + 1) * HD, :] for p in range(count)], axis=1)


def gate_up_kernel(place, r0, r1, r2, r3, own_w, other_w, own, sent1, sent2, sent3, total):
    acc = power = 0.0
    for j, rows in enumerate((r0, r1, r2, r3)):
        value = rows[...]
        weight = jnp.concatenate([weight_columns(w, j * PAYLOAD, 8) for w in (own_w, other_w)], axis=0)
        acc = acc + jnp.dot(value, weight, preferred_element_type=F32)
        value = value.astype(F32)
        power = power + jnp.sum(value * value, axis=1, keepdims=True)
    at = jnp.where(lax.rem(place[0], 2) == 1, 0, UNITS)
    lane = lax.broadcasted_iota(jnp.int32, acc.shape, 1)
    high = power.astype(BF).astype(F32)
    acc = jnp.where(lane == at, high, acc)
    acc = jnp.where(lane == at + 1, power - high, acc)
    total[...] = acc
    own[...] = total[pl.ds(place[1] * 48, 48), :]
    for j, sent in enumerate((sent1, sent2, sent3)):
        sent[...] = total[pl.ds(lax.rem(place[1] + j + 1, 4) * 48, 48), :].astype(BF)


def hidden_kernel(place, own, r1, r2, r3, out):
    total = own[...]
    for ref in (r1, r2, r3):
        total = total + ref[...].astype(F32)
    at = jnp.where(lax.rem(place[0], 2) == 1, 0, UNITS)
    gate, up = total[:, :WINDOW], total[:, WINDOW:]
    lane = lax.broadcasted_iota(jnp.int32, gate.shape, 1)
    marked = (lane == at) | (lane == at + 1)
    power = jnp.sum(jnp.where(marked, gate, 0.0), axis=1, keepdims=True)
    inv_rms = lax.rsqrt(power / D + 1e-05)
    gate, up = jnp.where(marked, 0.0, gate) * inv_rms, up * inv_rms
    out[...] = (gate / (1.0 + jnp.exp(-gate)) * up).astype(BF)


def down_kernel(h0, h1, h2, h3, own_w, other_w, own, sent1, sent2, sent3):
    hidden = jnp.concatenate([h[...] for h in (h0, h1, h2, h3)], axis=0)
    pieces = []
    for j in range(4):
        for w in (own_w, other_w):
            pieces.append(w[j * PAYLOAD + 8 * HD : (j + 1) * PAYLOAD, :])
    out = jnp.dot(hidden, jnp.concatenate(pieces, axis=1), preferred_element_type=F32)
    own[...] = out[:, : 2 * HD]
    for j, sent in enumerate((sent1, sent2, sent3)):
        sent[...] = out[:, (j + 1) * 2 * HD : (j + 2) * 2 * HD].astype(BF)


def add_kernel(own, r1, r2, r3, out, sent):
    total = own[...]
    for ref in (r1, r2, r3):
        total = total + ref[...].astype(F32)
    out[...] = total
    sent[...] = total.astype(BF)


def add_rolled_kernel(own, r1, r2, r3, out, sent):
    total = own[...]
    for j, ref in enumerate((r1, r2, r3)):
        received = ref[...].astype(F32)
        cut = 48 * (3 - j)
        total = total + jnp.concatenate([received[cut:], received[:cut]], axis=0)
    out[...] = total
    sent[...] = total.astype(BF)


def text_kernel(place, own, received, rows, own_w, other_w, enc_own, mine, sent1, sent2, sent3, whole, total):
    z = place[1]
    far = received[...].astype(F32)
    parts = []
    for k in range(4):
        parts += [far[48 * k + 24 : 48 * k + 48], far[48 * k : 48 * k + 24]]
    value = own[...] + jnp.concatenate(parts, axis=0)
    turned = [rows[pl.ds(pl.multiple_of(lax.rem(z + k, 4) * 48, 16), 48), :].astype(F32) for k in range(4)]
    value = value + jnp.concatenate(turned, axis=0)
    whole[...] = value
    enc_own[...] = whole[pl.ds(lax.rem(4 - z, 4) * 48, 24), :].astype(BF)
    base = 4 * PAYLOAD
    weight = jnp.concatenate([weight_columns(w, base, 6) for w in (own_w, other_w)], axis=0)
    total[...] = jnp.dot(value.astype(BF), weight, preferred_element_type=F32)
    for j, out in enumerate((mine, sent1, sent2, sent3)):
        block = total[pl.ds(lax.rem(place[0] + 4 + j - z, 4) * 48, 48), :]
        out[...] = block if j == 0 else block.astype(BF)


def text_norm_kernel(own, r1, r2, r3, gain, out):
    total = own[...]
    for ref in (r1, r2, r3):
        total = total + ref[...].astype(F32)
    for p in range(6):
        part = total[:, p * HD : (p + 1) * HD]
        if p < 3:
            part = part * lax.rsqrt(jnp.mean(part * part, axis=-1, keepdims=True) + 1e-06) * gain[...]
        out[:, p * HD : (p + 1) * HD] = part.astype(BF)


def qkv_kernel(order, *refs):
    blocks, refs = refs[:8], refs[8:]
    scale, shift, weight, q_gain, k_gain = refs[:5]
    q_out, kv_out, modulated = refs[-3:]
    rows, width = blocks[0].shape
    total = 8 * width
    half = rows // 2
    s = pl.program_id(0)

    @pl.when(s == 0)
    def _():
        for low in (0, half):
            load = lambda block: block[low : low + half, :].astype(F32)
            row_sum = 0.0
            for block in blocks:
                row_sum = row_sum + jnp.sum(load(block), axis=1, keepdims=True)
            mean = row_sum / total
            square_sum = 0.0
            for block in blocks:
                centred = load(block) - mean
                square_sum = square_sum + jnp.sum(centred * centred, axis=1, keepdims=True)
            inverse = lax.rsqrt(square_sum / total + 1e-06)
            for k, block in enumerate(blocks):
                at = order[k]
                gain = 1.0 + scale[pl.ds(at, 1), :]
                value = (load(block) - mean) * inverse * gain + shift[pl.ds(at, 1), :]
                modulated[low : low + half, pl.ds(pl.multiple_of(at * width, width), width)] = value.astype(BF)

    depth = modulated.shape[1]
    step = depth // 4
    projected = 0.0
    for c in range(4):
        part = jnp.concatenate([weight[0, h, c * step : (c + 1) * step, :] for h in range(3)], axis=1)
        projected = projected + jnp.dot(modulated[:, c * step : (c + 1) * step], part, preferred_element_type=F32)

    def normed(gain):
        parts = [projected[:, h * HD : (h + 1) * HD] for h in range(3)]
        parts = [p * lax.rsqrt(jnp.mean(p * p, axis=-1, keepdims=True) + 1e-06) * gain for p in parts]
        return jnp.concatenate(parts, axis=1).astype(BF)

    @pl.when(s == 0)
    def _():
        q_out[...] = normed(q_gain[...])

    @pl.when(s == 1)
    def _():
        kv_out[...] = normed(k_gain[...])

    @pl.when(s == 2)
    def _():
        kv_out[...] = projected.astype(BF)


def qkv(order, blocks, scale, shift, weight, q_gain, k_gain, rows, after):
    width = blocks[0].shape[1]
    depth = weight.shape[2]
    whole = lambda shape: pl.BlockSpec(shape, lambda s, o: (0,) * len(shape))
    return pl.pallas_call(
        qkv_kernel,
        grid_spec=pltpu.PrefetchScalarGridSpec(
            num_scalar_prefetch=1,
            grid=(3,),
            in_specs=[whole((rows, width))] * 8
            + [
                whole((8, width)),
                whole((8, width)),
                pl.BlockSpec((1, 3, depth, HD), lambda s, o: (s, 0, 0, 0)),
                whole((1, HD)),
                whole((1, HD)),
            ]
            + [glance(a) for a in after],
            out_specs=[
                whole((rows, 3 * HD)),
                pl.BlockSpec((rows, 3 * HD), lambda s, o: (0, jnp.maximum(s - 1, 0))),
            ],
            scratch_shapes=[pltpu.VMEM((rows, depth), BF)],
        ),
        out_shape=[jax.ShapeDtypeStruct((rows, 3 * HD), BF), jax.ShapeDtypeStruct((rows, 6 * HD), BF)],
        compiler_params=pltpu.CompilerParams(vmem_limit_bytes=40 * 2**20),
        cost_estimate=pl.CostEstimate(
            flops=2 * rows * depth * 9 * HD, bytes_accessed=2 * (depth * 9 * HD + 2 * rows * depth), transcendentals=0
        ),
        name="qkv",
    )(order, *blocks, scale, shift, weight, q_gain, k_gain, *after)


def attend_tile(query, pieces):
    top = total = out = None
    for keys, values in pieces:
        scores = lax.dot_general(query, keys, (((1,), (1,)), ((), ())), preferred_element_type=F32)
        here = jnp.max(scores, axis=1, keepdims=True)
        new_top = here if top is None else jnp.maximum(top, here)
        expon = jnp.exp2(scores - new_top)
        piece_sum = jnp.sum(expon, axis=1, keepdims=True)
        piece_out = jnp.dot(expon.astype(BF), values, preferred_element_type=F32)
        if top is None:
            total, out = piece_sum, piece_out
        else:
            factor = jnp.exp2(top - new_top)
            total, out = total * factor + piece_sum, out * factor + piece_out
        top = new_top
    return top, total, out


def attend_kernel(query_ref, key_ref, value_ref, after_ref, out_ref):
    rows = query_ref.shape[0]
    half = key_ref.shape[0] // 2
    pieces = [(key_ref[k * half : (k + 1) * half, :], value_ref[k * half : (k + 1) * half, :]) for k in (0, 1)]
    top, total, out = attend_tile(query_ref[...], pieces)
    out_ref[0:rows, :] = (out / total).astype(BF)
    level = top + jnp.log2(total)
    for b in range(rows // HD):
        across = jnp.transpose(jnp.broadcast_to(level[b * HD : (b + 1) * HD], (HD, HD)))[0:16, :]
        high = across.astype(BF).astype(F32)
        row_at = lax.broadcasted_iota(jnp.int32, (16, HD), 0)
        out_ref[rows + 16 * b : rows + 16 * (b + 1), :] = jnp.where(row_at == 1, across - high, high).astype(BF)


def attend(query, pairs, after):
    rows = query.shape[0]
    count = pairs.shape[0]
    out_rows = rows + 16 * (rows // HD)
    block = lambda at: pl.BlockSpec((count, HD), lambda h: (0, at + h))
    return pl.pallas_call(
        attend_kernel,
        grid=(3,),
        in_specs=[
            pl.BlockSpec((rows, HD), lambda h: (0, h)),
            block(0),
            block(3),
            glance(after),
        ],
        out_specs=pl.BlockSpec((out_rows, HD), lambda h: (0, h)),
        out_shape=jax.ShapeDtypeStruct((out_rows, 3 * HD), BF),
        compiler_params=pltpu.CompilerParams(vmem_limit_bytes=40 * 2**20),
        cost_estimate=pl.CostEstimate(
            flops=12 * rows * count * HD, bytes_accessed=12 * count * HD, transcendentals=3 * rows * count
        ),
        name="attend",
    )(query, pairs, pairs, after)


def combine_kernel(query_ref, key_a, key_b, value_a, value_b, *refs):
    parts, out_ref = refs[:-1], refs[-1]
    rows = query_ref.shape[0]
    keys = jnp.concatenate([key_a[...], key_b[...]], axis=0)
    values = jnp.concatenate([value_a[...], value_b[...]], axis=0)
    tile = HD
    for r in range(rows // tile):
        query = query_ref[r * tile : (r + 1) * tile, :]
        top, total, out = attend_tile(query, [(keys, values)])
        levels = []
        for part in parts:
            both = part[rows + 16 * r : rows + 16 * (r + 1), :].astype(F32)
            row_level = both[0:1, :] + both[1:2, :]
            levels.append(jnp.transpose(jnp.broadcast_to(row_level, (HD, tile))))
        new_top = top
        for level in levels:
            new_top = jnp.maximum(new_top, level)
        factor = jnp.exp2(top - new_top)
        total, out = total * factor, out * factor
        for part, level in zip(parts, levels):
            weight = jnp.exp2(level - new_top)
            total = total + weight
            out = out + weight * part[r * tile : (r + 1) * tile, :].astype(F32)
        out_ref[r * tile : (r + 1) * tile, :] = (out / total).astype(BF)


def combine(query, text_a, text_b, parts):
    rows = query.shape[0]
    count = text_a.shape[0]
    part_rows = parts[0].shape[0]
    block = lambda at: pl.BlockSpec((count, HD), lambda h: (0, at + h))
    return pl.pallas_call(
        combine_kernel,
        grid=(3,),
        in_specs=[pl.BlockSpec((rows, HD), lambda h: (0, h)), block(0), block(0), block(3), block(3)]
        + [pl.BlockSpec((part_rows, HD), lambda h: (0, h))] * len(parts),
        out_specs=pl.BlockSpec((rows, HD), lambda h: (0, h)),
        out_shape=jax.ShapeDtypeStruct((rows, 3 * HD), BF),
        compiler_params=pltpu.CompilerParams(vmem_limit_bytes=40 * 2**20),
        cost_estimate=pl.CostEstimate(
            flops=24 * rows * count * HD, bytes_accessed=6 * 8 * rows * HD, transcendentals=6 * rows * count
        ),
        name="combine",
    )(query, text_a, text_b, text_a, text_b, *parts)


def shards(
    enc_rows,
    enc_gain,
    w_gate,
    w_up,
    w_down,
    w_text_kv,
    text_gain,
    vid_rows,
    mod_shift,
    mod_scale,
    w_qkv,
    q_gain,
    k_gain,
):
    tp = lax.axis_index("tp")
    sp = lax.axis_index("sp")
    hi, x = tp // 4, tp % 4
    y, z, core = sp // 8, (sp // 2) % 4, sp % 2
    place = jnp.stack([y, z, core]).astype(jnp.int32)
    order = jnp.stack([(hi ^ a) * 4 + (x + j) % 4 for a in (0, 1) for j in range(4)]).astype(jnp.int32)

    rows = vid_rows.shape[0]
    (first,) = call(first_kernel, [((rows + 16, 3 * HD), BF)], [vid_rows, enc_rows], stream=True, name="first")
    spread = lambda value: [value] + [tp_send(value, dx=-j) for j in (1, 2, 3)]
    far = tp_send(first, dh=1)
    blocks = spread(first) + spread(far)

    payloads = call(
        prepare_kernel,
        [((PAYLOAD, HD), BF)] * 4 + [((6 * HD, HD), BF)],
        [w_gate, w_up, w_down, enc_gain[:, None], w_text_kv],
        scalars=place,
        stream=True,
        name="prepare",
    )
    own_w = [payloads[0]] + [sp_send(payloads[j], dy=-j) for j in (1, 2, 3)] + [payloads[4]]
    weight = jnp.transpose(w_qkv, (2, 1, 0, 3))
    mine, other, own_w = call(
        pick_kernel,
        [((192, HD), BF)] * 2 + [((4 * PAYLOAD + 6 * HD, HD), BF)],
        blocks + own_w,
        after=[weight],
        scalars=place,
        name="pick",
    )
    other_w = sp_send(own_w, dc=1)
    (rows_x,) = call(join_columns_kernel, [((192, 2 * HD), BF)], [mine, sp_send(other, dc=1)], name="join")
    gathered = [rows_x] + [sp_send(rows_x, dy=-j) for j in (1, 2, 3)]

    query, pairs = qkv(
        order,
        blocks,
        mod_scale.reshape(8, -1),
        mod_shift.reshape(8, -1),
        weight,
        (q_gain * (LOG2E / math.sqrt(HD)))[None],
        k_gain[None],
        rows,
        [rows_x],
    )
    groups = [[(yy * 4 + zz) * 2 + cc for yy in range(4) for cc in range(2)] for zz in range(4)]
    pairs = lax.all_gather(pairs, "sp", axis=0, tiled=True, axis_index_groups=groups)

    gate_up = call(
        gate_up_kernel,
        [((48, 2 * WINDOW), F32)] + [((48, 2 * WINDOW), BF)] * 3,
        gathered + [own_w, other_w],
        after=[query],
        scalars=place,
        scratch=[pltpu.VMEM((192, 2 * WINDOW), F32)],
        flops=2 * 192 * 1024 * 1024,
        name="gate_up",
    )
    received = [sp_send(gate_up[j], dz=j) for j in (1, 2, 3)]

    (hidden,) = call(
        hidden_kernel, [((48, WINDOW), BF)], [gate_up[0]] + received, scalars=place, name="hidden"
    )
    hidden = [hidden] + [sp_send(hidden, dz=-j) for j in (1, 2, 3)]

    shape = (192, 2 * HD)
    down = call(
        down_kernel,
        [(shape, F32)] + [(shape, BF)] * 3,
        hidden + [own_w, other_w],
        flops=2 * 192 * 512 * 1024,
        name="down",
    )
    received = [sp_send(down[j], dy=j) for j in (1, 2, 3)]
    (query_sent,) = call(copy_kernel, [(query.shape, BF)], [query], after=[down[0]], name="copy")
    far_query = {j: sp_send(query_sent, dz=-j) for j in (2, 1, 3)}
    own_part = attend(query, pairs, down[0])
    total, sent = call(
        add_kernel, [(shape, F32), (shape, BF)], [down[0]] + received, after=[own_part], name="add"
    )
    received = [tp_send(sent, dx=-j) for j in (1, 2, 3)]
    part = attend(far_query[2], pairs, total)
    parts = [own_part, sp_send(part, dz=2)]
    total, sent = call(add_rolled_kernel, [(shape, F32), (shape, BF)], [total] + received, after=[part], name="add")
    received = tp_send(sent, dh=1)
    part = attend(far_query[1], pairs, total)
    parts.append(sp_send(part, dz=1))

    shape = (48, 6 * HD)
    own_out, mine, *sent = call(
        text_kernel,
        [((24, 2 * HD), BF), (shape, F32)] + [(shape, BF)] * 3,
        [total, received, rows_x, own_w, other_w],
        after=[part],
        scalars=place,
        scratch=[pltpu.VMEM((192, 2 * HD), F32), pltpu.VMEM((192, 6 * HD), F32)],
        flops=2 * 192 * 256 * 768,
        name="text",
    )
    received = [sp_send(sent[j - 1], dy=j) for j in (1, 2, 3)]
    part = attend(far_query[3], pairs, mine)
    parts.append(sp_send(part, dz=3))
    total, sent = call(add_kernel, [(shape, F32), (shape, BF)], [mine] + received, after=[part], name="add")
    received = [sp_send(sent, dz=j) for j in (1, 2, 3)]
    (text,) = call(text_norm_kernel, [(shape, BF)], [total] + received + [text_gain[None]], after=[parts[1]], name="text_norm")
    text_all = [text] + [sp_send(text, dy=-j) for j in (1, 2, 3)]
    (text,) = call(join_rows_kernel, [((192, 6 * HD), BF)], text_all, after=[parts[2]], name="join")
    out = combine(query, text, sp_send(text, dc=1), parts)

    far_part = sp_send(own_out[:, HD:], dc=1)
    own_part = own_out[:, :HD]
    enc_mine = jnp.where(
        core == 0,
        jnp.concatenate([own_part, far_part], axis=0),
        jnp.concatenate([far_part, own_part], axis=0),
    )
    return (enc_mine, out.reshape(out.shape[0], 3, HD))


def solution(mesh):
    in_specs = (
        P("tp", "sp"),
        P("sp"),
        P("sp", "tp"),
        P("sp", "tp"),
        P("tp", "sp"),
        P("sp", "tp", None, None),
        P(),
        P("sp", "tp"),
        P(),
        P(),
        P(None, "tp", None, None),
        P(),
        P(),
    )
    out_specs = (P("tp", "sp"), P("sp", "tp", None))
    return jax.shard_map(shards, mesh=mesh, in_specs=in_specs, out_specs=out_specs, check_vma=False)
```

```python
import functools
import math

import jax
import jax.numpy as jnp
from jax import lax
from jax.experimental import pallas as pl
from jax.experimental.pallas import tpu as pltpu
from jax.sharding import PartitionSpec as P

D = 4096
BF = jnp.bfloat16
F32 = jnp.float32
HD = 128
LOG2E = 1.4426950408889634


def sp_send(value, dy=0, dz=0, dc=0):
    pairs = []
    for i in range(32):
        y, z, c = i // 8, (i // 2) % 4, i % 2
        pairs.append((i, (((y + dy) % 4) * 4 + (z + dz) % 4) * 2 + (c + dc) % 2))
    return lax.ppermute(value, "sp", pairs)


def tp_send(value, dh=0, dx=0):
    pairs = [(i, ((i // 4 + dh) % 2) * 4 + (i % 4 + dx) % 4) for i in range(8)]
    return lax.ppermute(value, "tp", pairs)


def glance(array):
    return pl.BlockSpec((1,) * (array.ndim - 2) + (16, HD), lambda *i: (0,) * array.ndim)


def rows_of(array, rows, at):
    return array, pl.BlockSpec((rows, array.shape[1]), lambda i: (at, 0))


def call(kernel, outs, ins, after=(), scalars=None, scratch=(), flops=0, name="step", stream=False):
    count = len(ins)
    shapes = [jax.ShapeDtypeStruct(shape, dtype) for shape, dtype in outs]
    lead = [] if scalars is None else [scalars]
    arrays, specs = [], []
    for value in ins:
        if isinstance(value, tuple):
            array, spec = value
        elif stream:
            array, spec = value, pl.BlockSpec(value.shape, lambda i, n=value.ndim: (0,) * n)
        else:
            array, spec = value, pl.BlockSpec(memory_space=pltpu.VMEM)
        arrays.append(array)
        specs.append(spec)

    def body(*refs):
        kept = refs[: len(lead) + count] + refs[len(lead) + count + len(after) :]
        kernel(*kept)

    size = sum(math.prod(a.shape) * a.dtype.itemsize for a in arrays + shapes)
    return pl.pallas_call(
        body,
        grid=(1,),
        in_specs=[pl.BlockSpec(memory_space=pltpu.SMEM)] * len(lead) + specs + [glance(a) for a in after],
        out_specs=[
            pl.BlockSpec(a.shape, lambda i, n=len(a.shape): (0,) * n) if stream else pl.BlockSpec(memory_space=pltpu.VMEM)
            for a in shapes
        ],
        out_shape=shapes,
        scratch_shapes=list(scratch),
        compiler_params=pltpu.CompilerParams(vmem_limit_bytes=(60 if stream else 16) * 2**20),
        cost_estimate=pl.CostEstimate(flops=flops, bytes_accessed=size, transcendentals=0),
        name=name,
    )(*lead, *arrays, *after)


UNITS = 448
WINDOW = 512
GATE_UP = 8 * HD
PAYLOAD = GATE_UP + WINDOW


def prepare_kernel(place, gate, up, down, gain, text, out0, out1, out2, out3):
    gain_column = gain[...]
    lane = lax.broadcasted_iota(jnp.int32, (HD, WINDOW), 1)
    row = lax.broadcasted_iota(jnp.int32, (WINDOW, HD), 0)
    for j, out in enumerate((out0, out1, out2, out3)):
        at = lax.rem(place[0] + 4 - j, 4)
        skip = lax.rem(at, 2) * 64
        start = pl.multiple_of(at * UNITS - skip, HD)
        for side, weight in enumerate((gate, up)):
            value = weight[:, pl.ds(start, WINDOW)].astype(F32) * gain_column
            value = jnp.where((lane >= skip) & (lane < skip + UNITS), value, 0.0).astype(BF)
            for p in range(4):
                out[(4 * side + p) * HD : (4 * side + p + 1) * HD, :] = value[:, p * HD : (p + 1) * HD]
        value = down[pl.ds(start, WINDOW), :].astype(F32)
        value = jnp.where((row >= skip) & (row < skip + UNITS), value, 0.0)
        out[8 * HD : PAYLOAD, :] = value.astype(BF)
    for s in range(2):
        for h in range(3):
            at = PAYLOAD + (3 * s + h) * HD
            out0[at : at + HD, :] = text[:, h, s, :]


def join_rows_kernel(*refs):
    out = refs[-1]
    at = 0
    for ref in refs[:-1]:
        out[at : at + ref.shape[0], :] = ref[...]
        at += ref.shape[0]


def copy_kernel(source, out):
    out[...] = source[...]


def first_kernel(video, own, out):
    rows = video.shape[0]
    out[0:rows, :] = video[...]
    for k in range(3):
        out[rows:, k * HD : (k + 1) * HD] = own[16 * k : 16 * (k + 1), :]


def pick_kernel(place, *refs):
    blocks, (mine, other) = refs[:8], refs[8:]
    first, second = [], []
    for j in range(4):
        for a in range(2):
            tail = blocks[a * 4 + j][...].astype(F32)
            part = jnp.concatenate([tail[:, k * HD : (k + 1) * HD] for k in range(3)], axis=0)
            first.append(part[:24])
            second.append(part[24:])
    first, second = jnp.concatenate(first, axis=0), jnp.concatenate(second, axis=0)
    is_first = place[2] == 0
    mine[...] = jnp.where(is_first, first, second).astype(BF)
    other[...] = jnp.where(is_first, second, first).astype(BF)


def join_columns_kernel(left, right, out):
    out[:, : left.shape[1]] = left[...]
    out[:, left.shape[1] :] = right[...]


def weight_columns(ref, at, count):
    return jnp.concatenate([ref[at + p * HD : at + (p + 1) * HD, :] for p in range(count)], axis=1)


def gate_up_kernel(place, *refs):
    gathered, own_w, other_w, (own, sent1, sent2, sent3, total) = refs[:4], refs[4:8], refs[8:12], refs[12:]
    acc = power = 0.0
    for rows, first, second in zip(gathered, own_w, other_w):
        value = rows[...]
        weight = jnp.concatenate([weight_columns(w, 0, 8) for w in (first, second)], axis=0)
        acc = acc + jnp.dot(value, weight, preferred_element_type=F32)
        value = value.astype(F32)
        power = power + jnp.sum(value * value, axis=1, keepdims=True)
    at = jnp.where(lax.rem(place[0], 2) == 1, 0, UNITS)
    lane = lax.broadcasted_iota(jnp.int32, acc.shape, 1)
    high = power.astype(BF).astype(F32)
    acc = jnp.where(lane == at, high, acc)
    acc = jnp.where(lane == at + 1, power - high, acc)
    total[...] = acc
    own[...] = total[pl.ds(place[1] * 48, 48), :]
    for j, sent in enumerate((sent1, sent2, sent3)):
        sent[...] = total[pl.ds(lax.rem(place[1] + j + 1, 4) * 48, 48), :].astype(BF)


def hidden_kernel(place, own, r1, r2, r3, out):
    total = own[...]
    for ref in (r1, r2, r3):
        total = total + ref[...].astype(F32)
    at = jnp.where(lax.rem(place[0], 2) == 1, 0, UNITS)
    gate, up = total[:, :WINDOW], total[:, WINDOW:]
    lane = lax.broadcasted_iota(jnp.int32, gate.shape, 1)
    marked = (lane == at) | (lane == at + 1)
    power = jnp.sum(jnp.where(marked, gate, 0.0), axis=1, keepdims=True)
    inv_rms = lax.rsqrt(power / D + 1e-05)
    gate, up = jnp.where(marked, 0.0, gate) * inv_rms, up * inv_rms
    out[...] = (gate / (1.0 + jnp.exp(-gate)) * up).astype(BF)


def down_kernel(*refs):
    blocks, own_w, other_w, (own, sent1, sent2, sent3) = refs[:4], refs[4:8], refs[8:12], refs[12:]
    hidden = jnp.concatenate([h[...] for h in blocks], axis=0)
    pieces = [w[...] for pair in zip(own_w, other_w) for w in pair]
    out = jnp.dot(hidden, jnp.concatenate(pieces, axis=1), preferred_element_type=F32)
    own[...] = out[:, : 2 * HD]
    for j, sent in enumerate((sent1, sent2, sent3)):
        sent[...] = out[:, (j + 1) * 2 * HD : (j + 2) * 2 * HD].astype(BF)


def add_kernel(own, r1, r2, r3, out, sent):
    total = own[...]
    for ref in (r1, r2, r3):
        total = total + ref[...].astype(F32)
    out[...] = total
    sent[...] = total.astype(BF)


def add_rolled_kernel(own, r1, r2, r3, out, sent):
    total = own[...]
    for j, ref in enumerate((r1, r2, r3)):
        received = ref[...].astype(F32)
        cut = 48 * (3 - j)
        total = total + jnp.concatenate([received[cut:], received[:cut]], axis=0)
    out[...] = total
    sent[...] = total.astype(BF)


def text_kernel(place, own, received, rows, own_w, other_w, enc_own, mine, sent1, sent2, sent3, whole, total):
    z = place[1]
    far = received[...].astype(F32)
    parts = []
    for k in range(4):
        parts += [far[48 * k + 24 : 48 * k + 48], far[48 * k : 48 * k + 24]]
    value = own[...] + jnp.concatenate(parts, axis=0)
    turned = [rows[pl.ds(pl.multiple_of(lax.rem(z + k, 4) * 48, 16), 48), :].astype(F32) for k in range(4)]
    value = value + jnp.concatenate(turned, axis=0)
    whole[...] = value
    enc_own[...] = whole[pl.ds(lax.rem(4 - z, 4) * 48, 24), :].astype(BF)
    weight = jnp.concatenate([weight_columns(w, 0, 6) for w in (own_w, other_w)], axis=0)
    total[...] = jnp.dot(value.astype(BF), weight, preferred_element_type=F32)
    for j, out in enumerate((mine, sent1, sent2, sent3)):
        block = total[pl.ds(lax.rem(place[0] + 4 + j - z, 4) * 48, 48), :]
        out[...] = block if j == 0 else block.astype(BF)


def text_norm_kernel(own, r1, r2, r3, gain, out):
    total = own[...]
    for ref in (r1, r2, r3):
        total = total + ref[...].astype(F32)
    for p in range(6):
        part = total[:, p * HD : (p + 1) * HD]
        if p < 3:
            part = part * lax.rsqrt(jnp.mean(part * part, axis=-1, keepdims=True) + 1e-06) * gain[...]
        out[:, p * HD : (p + 1) * HD] = part.astype(BF)


def qkv_kernel(order, *refs):
    blocks, refs = refs[:8], refs[8:]
    scale, shift, weight, q_gain, k_gain = refs[:5]
    q_out, kv_out, modulated = refs[-3:]
    rows, width = blocks[0].shape
    total = 8 * width
    half = rows // 2
    s = pl.program_id(0)

    @pl.when(s == 0)
    def _():
        for low in (0, half):
            load = lambda block: block[low : low + half, :].astype(F32)
            row_sum = 0.0
            for block in blocks:
                row_sum = row_sum + jnp.sum(load(block), axis=1, keepdims=True)
            mean = row_sum / total
            square_sum = 0.0
            for block in blocks:
                centred = load(block) - mean
                square_sum = square_sum + jnp.sum(centred * centred, axis=1, keepdims=True)
            inverse = lax.rsqrt(square_sum / total + 1e-06)
            for k, block in enumerate(blocks):
                at = order[k]
                gain = 1.0 + scale[pl.ds(at, 1), :]
                value = (load(block) - mean) * inverse * gain + shift[pl.ds(at, 1), :]
                modulated[low : low + half, pl.ds(pl.multiple_of(at * width, width), width)] = value.astype(BF)

    depth = modulated.shape[1]
    step = depth // 4
    projected = 0.0
    for c in range(4):
        part = jnp.concatenate([weight[0, h, c * step : (c + 1) * step, :] for h in range(3)], axis=1)
        projected = projected + jnp.dot(modulated[:, c * step : (c + 1) * step], part, preferred_element_type=F32)

    def normed(gain):
        parts = [projected[:, h * HD : (h + 1) * HD] for h in range(3)]
        parts = [p * lax.rsqrt(jnp.mean(p * p, axis=-1, keepdims=True) + 1e-06) * gain for p in parts]
        return jnp.concatenate(parts, axis=1).astype(BF)

    @pl.when(s == 0)
    def _():
        q_out[...] = normed(q_gain[...])

    @pl.when(s == 1)
    def _():
        kv_out[...] = normed(k_gain[...])

    @pl.when(s == 2)
    def _():
        kv_out[...] = projected.astype(BF)


def qkv(order, blocks, scale, shift, weight, q_gain, k_gain, rows, after):
    width = blocks[0].shape[1]
    depth = weight.shape[2]
    whole = lambda shape: pl.BlockSpec(shape, lambda s, o: (0,) * len(shape))
    return pl.pallas_call(
        qkv_kernel,
        grid_spec=pltpu.PrefetchScalarGridSpec(
            num_scalar_prefetch=1,
            grid=(3,),
            in_specs=[whole((rows, width))] * 8
            + [
                whole((8, width)),
                whole((8, width)),
                pl.BlockSpec((1, 3, depth, HD), lambda s, o: (s, 0, 0, 0)),
                whole((1, HD)),
                whole((1, HD)),
            ]
            + [glance(a) for a in after],
            out_specs=[
                whole((rows, 3 * HD)),
                pl.BlockSpec((rows, 3 * HD), lambda s, o: (0, jnp.maximum(s - 1, 0))),
            ],
            scratch_shapes=[pltpu.VMEM((rows, depth), BF)],
        ),
        out_shape=[jax.ShapeDtypeStruct((rows, 3 * HD), BF), jax.ShapeDtypeStruct((rows, 6 * HD), BF)],
        compiler_params=pltpu.CompilerParams(vmem_limit_bytes=60 * 2**20),
        cost_estimate=pl.CostEstimate(
            flops=2 * rows * depth * 9 * HD, bytes_accessed=2 * (depth * 9 * HD + 2 * rows * depth), transcendentals=0
        ),
        name="qkv",
    )(order, *blocks, scale, shift, weight, q_gain, k_gain, *after)


def attend_tile(query, pieces):
    top = total = out = None
    for keys, values in pieces:
        scores = lax.dot_general(query, keys, (((1,), (1,)), ((), ())), preferred_element_type=F32)
        here = jnp.max(scores, axis=1, keepdims=True)
        new_top = here if top is None else jnp.maximum(top, here)
        expon = jnp.exp2(scores - new_top)
        piece_sum = jnp.sum(expon, axis=1, keepdims=True)
        piece_out = jnp.dot(expon.astype(BF), values, preferred_element_type=F32)
        if top is None:
            total, out = piece_sum, piece_out
        else:
            factor = jnp.exp2(top - new_top)
            total, out = total * factor + piece_sum, out * factor + piece_out
        top = new_top
    return top, total, out


def attend_kernel(query_ref, key_ref, value_ref, after_ref, out_ref):
    rows = query_ref.shape[0]
    half = key_ref.shape[0] // 2
    pieces = [(key_ref[k * half : (k + 1) * half, :], value_ref[k * half : (k + 1) * half, :]) for k in (0, 1)]
    top, total, out = attend_tile(query_ref[...], pieces)
    out_ref[0:rows, :] = (out / total).astype(BF)
    level = top + jnp.log2(total)
    for b in range(rows // HD):
        across = jnp.transpose(jnp.broadcast_to(level[b * HD : (b + 1) * HD], (HD, HD)))[0:16, :]
        high = across.astype(BF).astype(F32)
        row_at = lax.broadcasted_iota(jnp.int32, (16, HD), 0)
        out_ref[rows + 16 * b : rows + 16 * (b + 1), :] = jnp.where(row_at == 1, across - high, high).astype(BF)


def attend(query, pairs, after):
    rows = query.shape[0]
    count = pairs.shape[0]
    out_rows = rows + 16 * (rows // HD)
    block = lambda at: pl.BlockSpec((count, HD), lambda h: (0, at + h))
    return pl.pallas_call(
        attend_kernel,
        grid=(3,),
        in_specs=[
            pl.BlockSpec((rows, HD), lambda h: (0, h)),
            block(0),
            block(3),
            glance(after),
        ],
        out_specs=pl.BlockSpec((out_rows, HD), lambda h: (0, h)),
        out_shape=jax.ShapeDtypeStruct((out_rows, 3 * HD), BF),
        compiler_params=pltpu.CompilerParams(vmem_limit_bytes=24 * 2**20),
        cost_estimate=pl.CostEstimate(
            flops=12 * rows * count * HD, bytes_accessed=12 * count * HD, transcendentals=3 * rows * count
        ),
        name="attend",
    )(query, pairs, pairs, after)


def combine_kernel(query_ref, key_a, key_b, value_a, value_b, *refs):
    parts, out_ref = refs[:-1], refs[-1]
    rows = query_ref.shape[0]
    keys = jnp.concatenate([key_a[...], key_b[...]], axis=0)
    values = jnp.concatenate([value_a[...], value_b[...]], axis=0)
    tile = HD
    for r in range(rows // tile):
        query = query_ref[r * tile : (r + 1) * tile, :]
        top, total, out = attend_tile(query, [(keys, values)])
        levels = []
        for part in parts:
            both = part[rows + 16 * r : rows + 16 * (r + 1), :].astype(F32)
            row_level = both[0:1, :] + both[1:2, :]
            levels.append(jnp.transpose(jnp.broadcast_to(row_level, (HD, tile))))
        new_top = top
        for level in levels:
            new_top = jnp.maximum(new_top, level)
        factor = jnp.exp2(top - new_top)
        total, out = total * factor, out * factor
        for part, level in zip(parts, levels):
            weight = jnp.exp2(level - new_top)
            total = total + weight
            out = out + weight * part[r * tile : (r + 1) * tile, :].astype(F32)
        out_ref[r * tile : (r + 1) * tile, :] = (out / total).astype(BF)


def combine(query, text_a, text_b, parts):
    rows = query.shape[0]
    count = text_a.shape[0]
    part_rows = parts[0].shape[0]
    block = lambda at: pl.BlockSpec((count, HD), lambda h: (0, at + h))
    return pl.pallas_call(
        combine_kernel,
        grid=(3,),
        in_specs=[pl.BlockSpec((rows, HD), lambda h: (0, h)), block(0), block(0), block(3), block(3)]
        + [pl.BlockSpec((part_rows, HD), lambda h: (0, h))] * len(parts),
        out_specs=pl.BlockSpec((rows, HD), lambda h: (0, h)),
        out_shape=jax.ShapeDtypeStruct((rows, 3 * HD), BF),
        compiler_params=pltpu.CompilerParams(vmem_limit_bytes=24 * 2**20),
        cost_estimate=pl.CostEstimate(
            flops=24 * rows * count * HD, bytes_accessed=6 * 8 * rows * HD, transcendentals=6 * rows * count
        ),
        name="combine",
    )(query, text_a, text_b, text_a, text_b, *parts)


def shards(
    enc_rows,
    enc_gain,
    w_gate,
    w_up,
    w_down,
    w_text_kv,
    text_gain,
    vid_rows,
    mod_shift,
    mod_scale,
    w_qkv,
    q_gain,
    k_gain,
):
    tp = lax.axis_index("tp")
    sp = lax.axis_index("sp")
    hi, x = tp // 4, tp % 4
    y, z, core = sp // 8, (sp // 2) % 4, sp % 2
    place = jnp.stack([y, z, core]).astype(jnp.int32)
    order = jnp.stack([(hi ^ a) * 4 + (x + j) % 4 for a in (0, 1) for j in range(4)]).astype(jnp.int32)

    rows = vid_rows.shape[0]
    (first,) = call(first_kernel, [((rows + 16, 3 * HD), BF)], [vid_rows, enc_rows], stream=True, name="first")
    spread = lambda value: [value] + [tp_send(value, dx=-j) for j in (1, 2, 3)]
    far = tp_send(first, dh=1)
    blocks = spread(first) + spread(far)

    payloads = call(
        prepare_kernel,
        [((PAYLOAD + 6 * HD, HD), BF)] + [((PAYLOAD, HD), BF)] * 3,
        [w_gate, w_up, w_down, enc_gain[:, None], w_text_kv],
        after=blocks[1:4] + [blocks[4]],
        scalars=place,
        stream=True,
        name="prepare",
    )
    own_w = [payloads[0]] + [sp_send(payloads[j], dy=-j) for j in (1, 2, 3)]
    other_w = [sp_send(w, dc=1) for w in own_w]
    weight = jnp.transpose(w_qkv, (2, 1, 0, 3))
    tails = [rows_of(block, 16, rows // 16) for block in blocks]
    mine, other = call(
        pick_kernel, [((192, HD), BF)] * 2, tails, after=[weight], scalars=place, stream=True, name="pick"
    )
    (rows_x,) = call(join_columns_kernel, [((192, 2 * HD), BF)], [mine, sp_send(other, dc=1)], name="join")
    gathered = [rows_x] + [sp_send(rows_x, dy=-j) for j in (1, 2, 3)]

    query, pairs = qkv(
        order,
        blocks,
        mod_scale.reshape(8, -1),
        mod_shift.reshape(8, -1),
        weight,
        (q_gain * (LOG2E / math.sqrt(HD)))[None],
        k_gain[None],
        rows,
        gathered[1:] + own_w[1:],
    )
    groups = [[(yy * 4 + zz) * 2 + cc for yy in range(4) for cc in range(2)] for zz in range(4)]
    pairs = lax.all_gather(pairs, "sp", axis=0, tiled=True, axis_index_groups=groups)

    gate_up = call(
        gate_up_kernel,
        [((48, 2 * WINDOW), F32)] + [((48, 2 * WINDOW), BF)] * 3,
        gathered + [rows_of(w, GATE_UP, 0) for w in own_w + other_w],
        after=[query],
        stream=True,
        scalars=place,
        scratch=[pltpu.VMEM((192, 2 * WINDOW), F32)],
        flops=2 * 192 * 1024 * 1024,
        name="gate_up",
    )
    received = [sp_send(gate_up[j], dz=j) for j in (1, 2, 3)]

    (hidden,) = call(
        hidden_kernel, [((48, WINDOW), BF)], [gate_up[0]] + received, scalars=place, name="hidden"
    )
    hidden = [hidden] + [sp_send(hidden, dz=-j) for j in (1, 2, 3)]

    shape = (192, 2 * HD)
    down = call(
        down_kernel,
        [(shape, F32)] + [(shape, BF)] * 3,
        hidden + [rows_of(w, WINDOW, GATE_UP // WINDOW) for w in own_w + other_w],
        stream=True,
        flops=2 * 192 * 512 * 1024,
        name="down",
    )
    received = [sp_send(down[j], dy=j) for j in (1, 2, 3)]
    (query_sent,) = call(copy_kernel, [(query.shape, BF)], [query], after=[down[0]], name="copy")
    far_query = {j: sp_send(query_sent, dz=-j) for j in (2, 1, 3)}
    own_part = attend(query, pairs, down[0])
    total, sent = call(
        add_kernel, [(shape, F32), (shape, BF)], [down[0]] + received, after=[own_part], name="add"
    )
    received = [tp_send(sent, dx=-j) for j in (1, 2, 3)]
    part = attend(far_query[2], pairs, total)
    parts = [own_part, sp_send(part, dz=2)]
    total, sent = call(add_rolled_kernel, [(shape, F32), (shape, BF)], [total] + received, after=[part], name="add")
    received = tp_send(sent, dh=1)
    part = attend(far_query[1], pairs, total)
    parts.append(sp_send(part, dz=1))

    shape = (48, 6 * HD)
    own_out, mine, *sent = call(
        text_kernel,
        [((24, 2 * HD), BF), (shape, F32)] + [(shape, BF)] * 3,
        [total, received, rows_x] + [rows_of(w[0], 6 * HD, PAYLOAD // (6 * HD)) for w in (own_w, other_w)],
        after=[part],
        scalars=place,
        scratch=[pltpu.VMEM((192, 2 * HD), F32), pltpu.VMEM((192, 6 * HD), F32)],
        flops=2 * 192 * 256 * 768,
        name="text",
    )
    received = [sp_send(sent[j - 1], dy=j) for j in (1, 2, 3)]
    part = attend(far_query[3], pairs, mine)
    parts.append(sp_send(part, dz=3))
    total, sent = call(add_kernel, [(shape, F32), (shape, BF)], [mine] + received, after=[part], name="add")
    received = [sp_send(sent, dz=j) for j in (1, 2, 3)]
    (text,) = call(text_norm_kernel, [(shape, BF)], [total] + received + [text_gain[None]], after=[parts[1]], name="text_norm")
    text_all = [text] + [sp_send(text, dy=-j) for j in (1, 2, 3)]
    (text,) = call(join_rows_kernel, [((192, 6 * HD), BF)], text_all, after=[parts[2]], name="join")
    out = combine(query, text, sp_send(text, dc=1), parts)

    far_part = sp_send(own_out[:, HD:], dc=1)
    own_part = own_out[:, :HD]
    enc_mine = jnp.where(
        core == 0,
        jnp.concatenate([own_part, far_part], axis=0),
        jnp.concatenate([far_part, own_part], axis=0),
    )
    return (enc_mine, out.reshape(out.shape[0], 3, HD))


def solution(mesh):
    in_specs = (
        P("tp", "sp"),
        P("sp"),
        P("sp", "tp"),
        P("sp", "tp"),
        P("tp", "sp"),
        P("sp", "tp", None, None),
        P(),
        P("sp", "tp"),
        P(),
        P(),
        P(None, "tp", None, None),
        P(),
        P(),
    )
    out_specs = (P("tp", "sp"), P("sp", "tp", None))
    return jax.shard_map(shards, mesh=mesh, in_specs=in_specs, out_specs=out_specs, check_vma=False)
```

```python
import functools
import math

import jax
import jax.numpy as jnp
from jax import lax
from jax.experimental import pallas as pl
from jax.experimental.pallas import tpu as pltpu
from jax.sharding import PartitionSpec as P

D = 4096
BF = jnp.bfloat16
F32 = jnp.float32
HD = 128
LOG2E = 1.4426950408889634


def sp_send(value, dy=0, dz=0, dc=0):
    pairs = []
    for i in range(32):
        y, z, c = i // 8, (i // 2) % 4, i % 2
        pairs.append((i, (((y + dy) % 4) * 4 + (z + dz) % 4) * 2 + (c + dc) % 2))
    return lax.ppermute(value, "sp", pairs)


def tp_send(value, dh=0, dx=0):
    pairs = [(i, ((i // 4 + dh) % 2) * 4 + (i % 4 + dx) % 4) for i in range(8)]
    return lax.ppermute(value, "tp", pairs)


def glance(array):
    return pl.BlockSpec((1,) * (array.ndim - 2) + (16, HD), lambda *i: (0,) * array.ndim)


def rows_of(array, rows, at):
    return array, pl.BlockSpec((rows, array.shape[1]), lambda i: (at, 0))


def call(kernel, outs, ins, after=(), scalars=None, scratch=(), flops=0, name="step", stream=False):
    count = len(ins)
    shapes = [jax.ShapeDtypeStruct(shape, dtype) for shape, dtype in outs]
    lead = [] if scalars is None else [scalars]
    arrays, specs = [], []
    for value in ins:
        if isinstance(value, tuple):
            array, spec = value
        elif stream:
            array, spec = value, pl.BlockSpec(value.shape, lambda i, n=value.ndim: (0,) * n)
        else:
            array, spec = value, pl.BlockSpec(memory_space=pltpu.VMEM)
        arrays.append(array)
        specs.append(spec)

    def body(*refs):
        kept = refs[: len(lead) + count] + refs[len(lead) + count + len(after) :]
        kernel(*kept)

    size = sum(math.prod(a.shape) * a.dtype.itemsize for a in arrays + shapes)
    return pl.pallas_call(
        body,
        grid=(1,),
        in_specs=[pl.BlockSpec(memory_space=pltpu.SMEM)] * len(lead) + specs + [glance(a) for a in after],
        out_specs=[
            pl.BlockSpec(a.shape, lambda i, n=len(a.shape): (0,) * n) if stream else pl.BlockSpec(memory_space=pltpu.VMEM)
            for a in shapes
        ],
        out_shape=shapes,
        scratch_shapes=list(scratch),
        compiler_params=pltpu.CompilerParams(vmem_limit_bytes=(60 if stream else 16) * 2**20),
        cost_estimate=pl.CostEstimate(flops=flops, bytes_accessed=size, transcendentals=0),
        name=name,
    )(*lead, *arrays, *after)


UNITS = 448
WINDOW = 512
GATE_UP = 8 * HD
PAYLOAD = GATE_UP + WINDOW


def prepare_kernel(place, gate, up, down, gain, text, out0, out1, out2, out3):
    gain_column = gain[...]
    lane = lax.broadcasted_iota(jnp.int32, (HD, WINDOW), 1)
    row = lax.broadcasted_iota(jnp.int32, (WINDOW, HD), 0)
    for j, out in enumerate((out0, out1, out2, out3)):
        at = lax.rem(place[0] + 4 - j, 4)
        skip = lax.rem(at, 2) * 64
        start = pl.multiple_of(at * UNITS - skip, HD)
        for side, weight in enumerate((gate, up)):
            value = weight[:, pl.ds(start, WINDOW)].astype(F32) * gain_column
            value = jnp.where((lane >= skip) & (lane < skip + UNITS), value, 0.0).astype(BF)
            for p in range(4):
                out[(4 * side + p) * HD : (4 * side + p + 1) * HD, :] = value[:, p * HD : (p + 1) * HD]
        value = down[pl.ds(start, WINDOW), :].astype(F32)
        value = jnp.where((row >= skip) & (row < skip + UNITS), value, 0.0)
        out[8 * HD : PAYLOAD, :] = value.astype(BF)
    for s in range(2):
        for h in range(3):
            at = PAYLOAD + (3 * s + h) * HD
            out0[at : at + HD, :] = text[:, h, s, :]


def join_rows_kernel(*refs):
    out = refs[-1]
    at = 0
    for ref in refs[:-1]:
        out[at : at + ref.shape[0], :] = ref[...]
        at += ref.shape[0]


def copy_kernel(source, out):
    out[...] = source[...]


def first_kernel(video, own, out):
    rows = video.shape[0]
    out[0:rows, :] = video[...]
    for k in range(3):
        out[rows:, k * HD : (k + 1) * HD] = own[16 * k : 16 * (k + 1), :]


def pick_kernel(place, *refs):
    blocks, (mine, other) = refs[:8], refs[8:]
    first, second = [], []
    for j in range(4):
        for a in range(2):
            tail = blocks[a * 4 + j][...].astype(F32)
            part = jnp.concatenate([tail[:, k * HD : (k + 1) * HD] for k in range(3)], axis=0)
            first.append(part[:24])
            second.append(part[24:])
    first, second = jnp.concatenate(first, axis=0), jnp.concatenate(second, axis=0)
    is_first = place[2] == 0
    mine[...] = jnp.where(is_first, first, second).astype(BF)
    other[...] = jnp.where(is_first, second, first).astype(BF)


def join_columns_kernel(left, right, out):
    out[:, : left.shape[1]] = left[...]
    out[:, left.shape[1] :] = right[...]


def weight_columns(ref, at, count):
    return jnp.concatenate([ref[at + p * HD : at + (p + 1) * HD, :] for p in range(count)], axis=1)


def gate_up_kernel(place, *refs):
    gathered, own_w, other_w, (own, sent1, sent2, sent3, total) = refs[:4], refs[4:8], refs[8:12], refs[12:]
    acc = power = 0.0
    for rows, first, second in zip(gathered, own_w, other_w):
        value = rows[...]
        weight = jnp.concatenate([weight_columns(w, 0, 8) for w in (first, second)], axis=0)
        acc = acc + jnp.dot(value, weight, preferred_element_type=F32)
        value = value.astype(F32)
        power = power + jnp.sum(value * value, axis=1, keepdims=True)
    at = jnp.where(lax.rem(place[0], 2) == 1, 0, UNITS)
    lane = lax.broadcasted_iota(jnp.int32, acc.shape, 1)
    high = power.astype(BF).astype(F32)
    acc = jnp.where(lane == at, high, acc)
    acc = jnp.where(lane == at + 1, power - high, acc)
    total[...] = acc
    own[...] = total[pl.ds(place[1] * 48, 48), :]
    for j, sent in enumerate((sent1, sent2, sent3)):
        sent[...] = total[pl.ds(lax.rem(place[1] + j + 1, 4) * 48, 48), :].astype(BF)


def hidden_kernel(place, own, r1, r2, r3, out):
    total = own[...]
    for ref in (r1, r2, r3):
        total = total + ref[...].astype(F32)
    at = jnp.where(lax.rem(place[0], 2) == 1, 0, UNITS)
    gate, up = total[:, :WINDOW], total[:, WINDOW:]
    lane = lax.broadcasted_iota(jnp.int32, gate.shape, 1)
    marked = (lane == at) | (lane == at + 1)
    power = jnp.sum(jnp.where(marked, gate, 0.0), axis=1, keepdims=True)
    inv_rms = lax.rsqrt(power / D + 1e-05)
    gate, up = jnp.where(marked, 0.0, gate) * inv_rms, up * inv_rms
    out[...] = (gate / (1.0 + jnp.exp(-gate)) * up).astype(BF)


def down_kernel(*refs):
    blocks, own_w, other_w, (own, sent1, sent2, sent3) = refs[:4], refs[4:8], refs[8:12], refs[12:]
    hidden = jnp.concatenate([h[...] for h in blocks], axis=0)
    pieces = [w[...] for pair in zip(own_w, other_w) for w in pair]
    out = jnp.dot(hidden, jnp.concatenate(pieces, axis=1), preferred_element_type=F32)
    own[...] = out[:, : 2 * HD]
    for j, sent in enumerate((sent1, sent2, sent3)):
        sent[...] = out[:, (j + 1) * 2 * HD : (j + 2) * 2 * HD].astype(BF)


def add_kernel(own, r1, r2, r3, out, sent):
    total = own[...]
    for ref in (r1, r2, r3):
        total = total + ref[...].astype(F32)
    out[...] = total
    sent[...] = total.astype(BF)


def add_rolled_kernel(own, r1, r2, r3, out, sent):
    total = own[...]
    for j, ref in enumerate((r1, r2, r3)):
        received = ref[...].astype(F32)
        cut = 48 * (3 - j)
        total = total + jnp.concatenate([received[cut:], received[:cut]], axis=0)
    out[...] = total
    sent[...] = total.astype(BF)


def text_kernel(place, own, received, rows, own_w, other_w, enc_own, mine, sent1, sent2, sent3, whole, total):
    z = place[1]
    far = received[...].astype(F32)
    parts = []
    for k in range(4):
        parts += [far[48 * k + 24 : 48 * k + 48], far[48 * k : 48 * k + 24]]
    value = own[...] + jnp.concatenate(parts, axis=0)
    turned = [rows[pl.ds(pl.multiple_of(lax.rem(z + k, 4) * 48, 16), 48), :].astype(F32) for k in range(4)]
    value = value + jnp.concatenate(turned, axis=0)
    whole[...] = value
    enc_own[...] = whole[pl.ds(lax.rem(4 - z, 4) * 48, 24), :].astype(BF)
    weight = jnp.concatenate([weight_columns(w, 0, 6) for w in (own_w, other_w)], axis=0)
    total[...] = jnp.dot(value.astype(BF), weight, preferred_element_type=F32)
    for j, out in enumerate((mine, sent1, sent2, sent3)):
        block = total[pl.ds(lax.rem(place[0] + 4 + j - z, 4) * 48, 48), :]
        out[...] = block if j == 0 else block.astype(BF)


def text_norm_kernel(own, r1, r2, r3, gain, out):
    total = own[...]
    for ref in (r1, r2, r3):
        total = total + ref[...].astype(F32)
    for p in range(6):
        part = total[:, p * HD : (p + 1) * HD]
        if p < 3:
            part = part * lax.rsqrt(jnp.mean(part * part, axis=-1, keepdims=True) + 1e-06) * gain[...]
        out[:, p * HD : (p + 1) * HD] = part.astype(BF)


def qkv_kernel(order, *refs):
    blocks, refs = refs[:8], refs[8:]
    scale, shift, weight, q_gain, k_gain = refs[:5]
    q_out, kv_out, modulated = refs[-3:]
    rows, width = blocks[0].shape
    total = 8 * width
    half = rows // 2
    s = pl.program_id(0)

    @pl.when(s == 0)
    def _():
        for low in (0, half):
            load = lambda block: block[low : low + half, :].astype(F32)
            row_sum = 0.0
            for block in blocks:
                row_sum = row_sum + jnp.sum(load(block), axis=1, keepdims=True)
            mean = row_sum / total
            square_sum = 0.0
            for block in blocks:
                centred = load(block) - mean
                square_sum = square_sum + jnp.sum(centred * centred, axis=1, keepdims=True)
            inverse = lax.rsqrt(square_sum / total + 1e-06)
            for k, block in enumerate(blocks):
                at = order[k]
                gain = 1.0 + scale[pl.ds(at, 1), :]
                value = (load(block) - mean) * inverse * gain + shift[pl.ds(at, 1), :]
                modulated[low : low + half, pl.ds(pl.multiple_of(at * width, width), width)] = value.astype(BF)

    depth = modulated.shape[1]
    step = depth // 4
    projected = 0.0
    for c in range(4):
        part = jnp.concatenate([weight[0, h, c * step : (c + 1) * step, :] for h in range(3)], axis=1)
        projected = projected + jnp.dot(modulated[:, c * step : (c + 1) * step], part, preferred_element_type=F32)

    def normed(gain):
        parts = [projected[:, h * HD : (h + 1) * HD] for h in range(3)]
        parts = [p * lax.rsqrt(jnp.mean(p * p, axis=-1, keepdims=True) + 1e-06) * gain for p in parts]
        return jnp.concatenate(parts, axis=1).astype(BF)

    @pl.when(s == 0)
    def _():
        q_out[...] = normed(q_gain[...])

    @pl.when(s == 1)
    def _():
        kv_out[...] = normed(k_gain[...])

    @pl.when(s == 2)
    def _():
        kv_out[...] = projected.astype(BF)


def qkv(order, blocks, scale, shift, weight, q_gain, k_gain, rows, after):
    width = blocks[0].shape[1]
    depth = weight.shape[2]
    whole = lambda shape: pl.BlockSpec(shape, lambda s, o: (0,) * len(shape))
    return pl.pallas_call(
        qkv_kernel,
        grid_spec=pltpu.PrefetchScalarGridSpec(
            num_scalar_prefetch=1,
            grid=(3,),
            in_specs=[whole((rows, width))] * 8
            + [
                whole((8, width)),
                whole((8, width)),
                pl.BlockSpec((1, 3, depth, HD), lambda s, o: (s, 0, 0, 0)),
                whole((1, HD)),
                whole((1, HD)),
            ]
            + [glance(a) for a in after],
            out_specs=[
                whole((rows, 3 * HD)),
                pl.BlockSpec((rows, 3 * HD), lambda s, o: (0, jnp.maximum(s - 1, 0))),
            ],
            scratch_shapes=[pltpu.VMEM((rows, depth), BF)],
        ),
        out_shape=[jax.ShapeDtypeStruct((rows, 3 * HD), BF), jax.ShapeDtypeStruct((rows, 6 * HD), BF)],
        compiler_params=pltpu.CompilerParams(vmem_limit_bytes=60 * 2**20),
        cost_estimate=pl.CostEstimate(
            flops=2 * rows * depth * 9 * HD, bytes_accessed=2 * (depth * 9 * HD + 2 * rows * depth), transcendentals=0
        ),
        name="qkv",
    )(order, *blocks, scale, shift, weight, q_gain, k_gain, *after)


def attend_tile(query, pieces):
    top = total = out = None
    for keys, values in pieces:
        scores = lax.dot_general(query, keys, (((1,), (1,)), ((), ())), preferred_element_type=F32)
        here = jnp.max(scores, axis=1, keepdims=True)
        new_top = here if top is None else jnp.maximum(top, here)
        expon = jnp.exp2(scores - new_top)
        piece_sum = jnp.sum(expon, axis=1, keepdims=True)
        piece_out = jnp.dot(expon.astype(BF), values, preferred_element_type=F32)
        if top is None:
            total, out = piece_sum, piece_out
        else:
            factor = jnp.exp2(top - new_top)
            total, out = total * factor + piece_sum, out * factor + piece_out
        top = new_top
    return top, total, out


def attend_kernel(query_ref, key_ref, value_ref, after_ref, out_ref):
    rows = query_ref.shape[0]
    half = key_ref.shape[0] // 2
    pieces = [(key_ref[k * half : (k + 1) * half, :], value_ref[k * half : (k + 1) * half, :]) for k in (0, 1)]
    top, total, out = attend_tile(query_ref[...], pieces)
    out_ref[0:rows, :] = (out / total).astype(BF)
    level = top + jnp.log2(total)
    for b in range(rows // HD):
        across = jnp.transpose(jnp.broadcast_to(level[b * HD : (b + 1) * HD], (HD, HD)))[0:16, :]
        high = across.astype(BF).astype(F32)
        row_at = lax.broadcasted_iota(jnp.int32, (16, HD), 0)
        out_ref[rows + 16 * b : rows + 16 * (b + 1), :] = jnp.where(row_at == 1, across - high, high).astype(BF)


def attend(query, pairs, after):
    rows = query.shape[0]
    count = pairs.shape[0]
    out_rows = rows + 16 * (rows // HD)
    block = lambda at: pl.BlockSpec((count, HD), lambda h: (0, at + h))
    return pl.pallas_call(
        attend_kernel,
        grid=(3,),
        in_specs=[
            pl.BlockSpec((rows, HD), lambda h: (0, h)),
            block(0),
            block(3),
            glance(after),
        ],
        out_specs=pl.BlockSpec((out_rows, HD), lambda h: (0, h)),
        out_shape=jax.ShapeDtypeStruct((out_rows, 3 * HD), BF),
        compiler_params=pltpu.CompilerParams(vmem_limit_bytes=24 * 2**20),
        cost_estimate=pl.CostEstimate(
            flops=12 * rows * count * HD, bytes_accessed=12 * count * HD, transcendentals=3 * rows * count
        ),
        name="attend",
    )(query, pairs, pairs, after)


def combine_kernel(query_ref, key_a, key_b, value_a, value_b, *refs):
    parts, out_ref = refs[:-1], refs[-1]
    rows = query_ref.shape[0]
    keys = jnp.concatenate([key_a[...], key_b[...]], axis=0)
    values = jnp.concatenate([value_a[...], value_b[...]], axis=0)
    tile = HD
    for r in range(rows // tile):
        query = query_ref[r * tile : (r + 1) * tile, :]
        top, total, out = attend_tile(query, [(keys, values)])
        levels = []
        for part in parts:
            both = part[rows + 16 * r : rows + 16 * (r + 1), :].astype(F32)
            row_level = both[0:1, :] + both[1:2, :]
            levels.append(jnp.transpose(jnp.broadcast_to(row_level, (HD, tile))))
        new_top = top
        for level in levels:
            new_top = jnp.maximum(new_top, level)
        factor = jnp.exp2(top - new_top)
        total, out = total * factor, out * factor
        for part, level in zip(parts, levels):
            weight = jnp.exp2(level - new_top)
            total = total + weight
            out = out + weight * part[r * tile : (r + 1) * tile, :].astype(F32)
        out_ref[r * tile : (r + 1) * tile, :] = (out / total).astype(BF)


def combine(query, text_a, text_b, parts):
    rows = query.shape[0]
    count = text_a.shape[0]
    part_rows = parts[0].shape[0]
    block = lambda at: pl.BlockSpec((count, HD), lambda h: (0, at + h))
    return pl.pallas_call(
        combine_kernel,
        grid=(3,),
        in_specs=[pl.BlockSpec((rows, HD), lambda h: (0, h)), block(0), block(0), block(3), block(3)]
        + [pl.BlockSpec((part_rows, HD), lambda h: (0, h))] * len(parts),
        out_specs=pl.BlockSpec((rows, HD), lambda h: (0, h)),
        out_shape=jax.ShapeDtypeStruct((rows, 3 * HD), BF),
        compiler_params=pltpu.CompilerParams(vmem_limit_bytes=24 * 2**20),
        cost_estimate=pl.CostEstimate(
            flops=24 * rows * count * HD, bytes_accessed=6 * 8 * rows * HD, transcendentals=6 * rows * count
        ),
        name="combine",
    )(query, text_a, text_b, text_a, text_b, *parts)


def shards(
    enc_rows,
    enc_gain,
    w_gate,
    w_up,
    w_down,
    w_text_kv,
    text_gain,
    vid_rows,
    mod_shift,
    mod_scale,
    w_qkv,
    q_gain,
    k_gain,
):
    tp = lax.axis_index("tp")
    sp = lax.axis_index("sp")
    hi, x = tp // 4, tp % 4
    y, z, core = sp // 8, (sp // 2) % 4, sp % 2
    place = jnp.stack([y, z, core]).astype(jnp.int32)
    order = jnp.stack([(hi ^ a) * 4 + (x + j) % 4 for a in (0, 1) for j in range(4)]).astype(jnp.int32)

    rows = vid_rows.shape[0]
    (first,) = call(first_kernel, [((rows + 16, 3 * HD), BF)], [vid_rows, enc_rows], stream=True, name="first")
    spread = lambda value: [value] + [tp_send(value, dx=-j) for j in (1, 2, 3)]
    far = tp_send(first, dh=1)
    blocks = spread(first) + spread(far)

    payloads = call(
        prepare_kernel,
        [((PAYLOAD + 6 * HD, HD), BF)] + [((PAYLOAD, HD), BF)] * 3,
        [w_gate, w_up, w_down, enc_gain[:, None], w_text_kv],
        after=[blocks[4]],
        scalars=place,
        stream=True,
        name="prepare",
    )
    own_w = [payloads[0]] + [sp_send(payloads[j], dy=-j) for j in (1, 2, 3)]
    other_w = [sp_send(w, dc=1) for w in own_w]
    weight = jnp.transpose(w_qkv, (2, 1, 0, 3))
    tails = [rows_of(block, 16, rows // 16) for block in blocks]
    mine, other = call(
        pick_kernel, [((192, HD), BF)] * 2, tails, after=[weight], scalars=place, stream=True, name="pick"
    )
    (rows_x,) = call(join_columns_kernel, [((192, 2 * HD), BF)], [mine, sp_send(other, dc=1)], name="join")
    gathered = [rows_x] + [sp_send(rows_x, dy=-j) for j in (1, 2, 3)]

    query, pairs = qkv(
        order,
        blocks,
        mod_scale.reshape(8, -1),
        mod_shift.reshape(8, -1),
        weight,
        (q_gain * (LOG2E / math.sqrt(HD)))[None],
        k_gain[None],
        rows,
        gathered[1:] + own_w[1:],
    )
    groups = [[(yy * 4 + zz) * 2 + cc for yy in range(4) for cc in range(2)] for zz in range(4)]
    pairs = lax.all_gather(pairs, "sp", axis=0, tiled=True, axis_index_groups=groups)

    gate_up = call(
        gate_up_kernel,
        [((48, 2 * WINDOW), F32)] + [((48, 2 * WINDOW), BF)] * 3,
        gathered + [rows_of(w, GATE_UP, 0) for w in own_w + other_w],
        after=[query],
        stream=True,
        scalars=place,
        scratch=[pltpu.VMEM((192, 2 * WINDOW), F32)],
        flops=2 * 192 * 1024 * 1024,
        name="gate_up",
    )
    received = [sp_send(gate_up[j], dz=j) for j in (1, 2, 3)]

    (hidden,) = call(
        hidden_kernel, [((48, WINDOW), BF)], [gate_up[0]] + received, scalars=place, name="hidden"
    )
    hidden = [hidden] + [sp_send(hidden, dz=-j) for j in (1, 2, 3)]

    shape = (192, 2 * HD)
    down = call(
        down_kernel,
        [(shape, F32)] + [(shape, BF)] * 3,
        hidden + [rows_of(w, WINDOW, GATE_UP // WINDOW) for w in own_w + other_w],
        stream=True,
        flops=2 * 192 * 512 * 1024,
        name="down",
    )
    received = [sp_send(down[j], dy=j) for j in (1, 2, 3)]
    (query_sent,) = call(copy_kernel, [(query.shape, BF)], [query], after=[down[0]], name="copy")
    far_query = {j: sp_send(query_sent, dz=-j) for j in (2, 1, 3)}
    own_part = attend(query, pairs, down[0])
    total, sent = call(
        add_kernel, [(shape, F32), (shape, BF)], [down[0]] + received, after=[own_part], name="add"
    )
    received = [tp_send(sent, dx=-j) for j in (1, 2, 3)]
    part = attend(far_query[2], pairs, total)
    parts = [own_part, sp_send(part, dz=2)]
    total, sent = call(add_rolled_kernel, [(shape, F32), (shape, BF)], [total] + received, after=[part], name="add")
    received = tp_send(sent, dh=1)
    part = attend(far_query[1], pairs, total)
    parts.append(sp_send(part, dz=1))

    shape = (48, 6 * HD)
    own_out, mine, *sent = call(
        text_kernel,
        [((24, 2 * HD), BF), (shape, F32)] + [(shape, BF)] * 3,
        [total, received, rows_x] + [rows_of(w[0], 6 * HD, PAYLOAD // (6 * HD)) for w in (own_w, other_w)],
        after=[part],
        scalars=place,
        scratch=[pltpu.VMEM((192, 2 * HD), F32), pltpu.VMEM((192, 6 * HD), F32)],
        flops=2 * 192 * 256 * 768,
        name="text",
    )
    received = [sp_send(sent[j - 1], dy=j) for j in (1, 2, 3)]
    part = attend(far_query[3], pairs, mine)
    parts.append(sp_send(part, dz=3))
    total, sent = call(add_kernel, [(shape, F32), (shape, BF)], [mine] + received, after=[part], name="add")
    received = [sp_send(sent, dz=j) for j in (1, 2, 3)]
    (text,) = call(text_norm_kernel, [(shape, BF)], [total] + received + [text_gain[None]], after=[parts[1]], name="text_norm")
    text_all = [text] + [sp_send(text, dy=-j) for j in (1, 2, 3)]
    (text,) = call(join_rows_kernel, [((192, 6 * HD), BF)], text_all, after=[parts[2]], name="join")
    out = combine(query, text, sp_send(text, dc=1), parts)

    far_part = sp_send(own_out[:, HD:], dc=1)
    own_part = own_out[:, :HD]
    enc_mine = jnp.where(
        core == 0,
        jnp.concatenate([own_part, far_part], axis=0),
        jnp.concatenate([far_part, own_part], axis=0),
    )
    return (enc_mine, out.reshape(out.shape[0], 3, HD))


def solution(mesh):
    in_specs = (
        P("tp", "sp"),
        P("sp"),
        P("sp", "tp"),
        P("sp", "tp"),
        P("tp", "sp"),
        P("sp", "tp", None, None),
        P(),
        P("sp", "tp"),
        P(),
        P(),
        P(None, "tp", None, None),
        P(),
        P(),
    )
    out_specs = (P("tp", "sp"), P("sp", "tp", None))
    return jax.shard_map(shards, mesh=mesh, in_specs=in_specs, out_specs=out_specs, check_vma=False)
```
